128 devices in a mesh: fsdp: 8 (over x_hi, y), ctx: 8 (over z, x_lo), tp: 2 (over core).
Axes of the slice: x: 4 (x_hi: 2, x_lo: 2; x = x_hi * 2 + x_lo), y: 4, z: 4, core: 2. Of those that a mesh axis runs over, the one named last changes fastest.
Arguments:
- tokens: float32 [8192, 1536], P(('fsdp', 'ctx')), may hold values from -6 to 6
- cotangent: float32 [8192, 1536], P(('fsdp', 'ctx')), may hold values from -6 to 6
- norm_attn: bfloat16 [1536], P('fsdp'), may hold values from 0.5 to 1.5
- qkv_weight: bfloat16 [1536, 2048], P('fsdp', 'tp'), may hold values from -0.15625 to 0.15625
- qkv_bias: bfloat16 [2, 1024], P('tp', 'fsdp'), may hold values from -3 to 3
- out_weight: bfloat16 [1536, 1536], P('tp', 'fsdp'), may hold values from -0.875 to 0.875
- norm_mlp: bfloat16 [1536], P('fsdp'), may hold values from 0.5 to 1.5
- gate_up_weight: bfloat16 [1536, 2, 8960], P('fsdp', None, 'tp'), may hold values from -0.15625 to 0.15625
- down_weight: bfloat16 [8960, 1536], P('tp', 'fsdp'), may hold values from -0.125 to 0.125
- lengths: int32 [8, 4], P('fsdp'), may hold values from 1 to 512, 1024 in all within a row
- deal: int32 [8, 1024], P('fsdp'), may hold values from 0 to 1023, as said below
Outputs:
- output: float32 [8192, 1536], P(('fsdp', 'ctx'))
- grad_tokens: float32 [8192, 1536], P(('fsdp', 'ctx'))
- grad_norm_attn: float32 [1536], P('fsdp')
- grad_qkv_weight: float32 [1536, 2048], P('fsdp', 'tp')
- grad_qkv_bias: float32 [2, 896], P('tp', 'fsdp')
- grad_value_bias: float32 [2, 128], P('tp', 'fsdp')
- grad_out_weight: float32 [1536, 1536], P('tp', 'fsdp')
- grad_norm_mlp: float32 [1536], P('fsdp')
- grad_gate_up_weight: float32 [1536, 2, 8960], P('fsdp', None, 'tp')
- grad_down_weight: float32 [8960, 1536], P('tp', 'fsdp')
The draws below stay inside these ranges and needn't reach their ends.
Inputs may be any that keep to these rules, and one draw needn't show every extreme that they name: `lengths`: each row sums to 1024; its largest entry is 512. `deal`: each row is a permutation of the places of the pack; entry c * 128 + r lies between r * 8 and r * 8 + 7.
All inputs are finite; a program needn't handle non-finite values.
Results may differ from the reference program's by a relative error of at most 0.035.
Values may be sent and summed in bfloat16 or wider, within the bound.
No kernel may reach another device: no remote copies, remote signals or barrier semaphores. Data moves between devices by JAX's collectives and lax.ppermute only.
A program may use at most 256 MiB of HBM per device.

```python
import math
import jax
import jax.numpy as jnp
import numpy as np
from jax import lax

D = 1536
HEAD = 128
HEADS = 12
KV_HEADS = 2
FF = 8960
TOK_DEV = 128
SEQS = 4
GROUP_Q = 6
QKV_COLS = 1024
SPREAD = 8
PACK = 1024
GROUPS = 8
TOKENS = 8192


def draw_deal(key, part):
    key = jax.random.fold_in(key, 7)
    subkeys = jax.random.split(key, GROUPS * TOK_DEV)
    orders = jax.vmap(lambda subkey: jax.random.permutation(subkey, SPREAD))(subkeys)
    orders = orders.reshape(GROUPS, TOK_DEV, SPREAD).astype(jnp.int32)
    rounds = jnp.arange(TOK_DEV, dtype=jnp.int32)[None, :, None] * SPREAD
    places = rounds + orders
    return jnp.transpose(places, (0, 2, 1)).reshape(GROUPS, PACK).astype(jnp.int32)


def shard_levels(own_key, extent, cuts, smallest, top_value):
    level = 1.0
    for dim, blocks in cuts:
        steps = jax.random.uniform(jax.random.fold_in(jax.random.fold_in(own_key, 6), dim), (blocks,), jnp.float32, smallest / len(cuts), top_value / len(cuts))
        level = level * jnp.repeat(jnp.exp(steps), extent[dim] // blocks).reshape((-1,) + (1,) * (len(extent) - 1 - dim))
    return level


def length_profile(amount, total, bound, skew):
    weights = [(1 << 20) // math.isqrt(grade ** skew) + 1 for grade in range(2, amount + 1)]
    surplus, counts = total - bound - (amount - 1), [1] * (amount - 1)
    while surplus > 0:
        free = [i for i in range(amount - 1) if counts[i] < bound]
        pool, budget = sum([weights[i] for i in free]), surplus
        for i in free:
            more = min(bound - counts[i], max(1, budget * weights[i] // pool), surplus)
            counts[i] = counts[i] + more
            surplus = surplus - more
    return np.array([bound] + counts)


def ragged_sizes(own_key, amount, total, most, slope):
    if amount == 2:
        one = jax.random.randint(own_key, (), max(1, total - most), min(most, total - 1) + 1)
        return jnp.stack([one, total - one])
    sizes = jnp.asarray(length_profile(amount, total, most, slope), jnp.int32)
    twos = (amount - 1) // 2
    source_of, receiver = sizes[1:1 + 2 * twos:2], sizes[2:2 + 2 * twos:2]
    slack = jnp.minimum(source_of - 1, most - receiver)
    passed = jax.random.randint(jax.random.fold_in(own_key, 1), (twos,), 0, 1 << 20) % (slack + 1)
    sizes = sizes.at[1:1 + 2 * twos:2].set(source_of - passed).at[2:2 + 2 * twos:2].set(receiver + passed)
    return sizes[jax.random.permutation(jax.random.fold_in(own_key, 2), amount)]


def bell_draw(rng, extent, scale, reach, cuts=(), kind=jnp.bfloat16):
    level = shard_levels(rng, extent, cuts, -0.22, 0.18) if cuts else 1.0
    values = jax.random.normal(rng, extent, jnp.float32) * scale * level
    return jnp.minimum(jnp.maximum(values, -reach), reach).astype(kind)


def setup_inputs(seed: int = 0) -> dict:
    arg_keys = jax.random.split(jax.random.key(seed), 12)
    tokens = bell_draw(arg_keys[0], (TOKENS, D), 1.0, 6.0, ((0, 64),), jnp.float32)
    cotangent = bell_draw(arg_keys[1], (TOKENS, D), 1.0, 6.0, ((0, 64),), jnp.float32)
    norm_attn = jnp.clip(1.0 + 0.1 * jax.random.normal(arg_keys[2], (D,), jnp.float32), 0.5, 1.5).astype(jnp.bfloat16)
    qkv_weight = bell_draw(arg_keys[3], (D, KV_HEADS * QKV_COLS), D ** -0.5, 0.15625, ((0, 8), (1, 2)))
    qkv_bias = bell_draw(arg_keys[4], (KV_HEADS, QKV_COLS), 0.5, 3.0, ((0, 2), (1, 8)))
    out_weight = bell_draw(arg_keys[5], (HEADS * HEAD, D), (GROUP_Q * HEAD // 16) ** -0.5, 0.875, ((0, 2), (1, 8)))
    norm_mlp = jnp.clip(1.0 + 0.1 * jax.random.normal(arg_keys[6], (D,), jnp.float32), 0.5, 1.5).astype(jnp.bfloat16)
    gate_up_weight = bell_draw(arg_keys[7], (D, 2, FF), D ** -0.5, 0.15625, ((0, 8), (2, 2)))
    down_weight = bell_draw(arg_keys[8], (FF, D), (FF // 4) ** -0.5, 0.125, ((0, 2), (1, 8)))
    lengths = jax.vmap(lambda own: ragged_sizes(own, SEQS, PACK, PACK // 2, 2))(jax.random.split(arg_keys[9], GROUPS)).reshape((GROUPS, SEQS)).astype(jnp.int32)
    deal = draw_deal(jax.random.fold_in(arg_keys[11], 71), 0)
    return dict(tokens=tokens, cotangent=cotangent, norm_attn=norm_attn, qkv_weight=qkv_weight, qkv_bias=qkv_bias, out_weight=out_weight, norm_mlp=norm_mlp, gate_up_weight=gate_up_weight, down_weight=down_weight, lengths=lengths, deal=deal)


EPS = 1e-06
THETA = 1000000.0

@jax.custom_vjp
def low(v):
    return lax.optimization_barrier(v.astype(jnp.bfloat16)).astype(jnp.float32)

@jax.custom_vjp
def low_back(v):
    return v

def low_keep(v):
    return (low(v), None)

def low_pass(kept, grad):
    return (grad,)

def back_keep(v):
    return (v, None)

def back_low(kept, grad):
    return (low(grad),)
low.defvjp(low_keep, low_pass)
low_back.defvjp(back_keep, back_low)

def segment_of(places, seq_lengths):
    ends = jnp.cumsum(seq_lengths).astype(jnp.int32)
    starts = ends - seq_lengths
    inside = ((places[:, None] >= starts[None, :]) & (places[:, None] < ends[None, :])).astype(jnp.int32)
    segment = lax.optimization_barrier(jnp.sum(inside * jnp.arange(seq_lengths.shape[0], dtype=jnp.int32)[None, :], axis=1))
    offset = places - lax.optimization_barrier(jnp.sum(inside * starts[None, :], axis=1))
    return (segment, offset)

def rotary(offset, width):
    half = width // 2
    freqs = THETA ** (-(2.0 * jnp.arange(half, dtype=jnp.float32)) / width)
    angle = offset.astype(jnp.float32)[:, None] * freqs[None, :]
    cosine = jnp.concatenate([jnp.cos(angle), jnp.cos(angle)], axis=1)
    sine = jnp.concatenate([jnp.sin(angle), jnp.sin(angle)], axis=1)
    return (cosine, sine)

def rotate_half(values):
    half = values.shape[-1] // 2
    return jnp.concatenate([-values[..., half:], values[..., :half]], axis=-1)

def rope_apply(values, cosine, sine):
    return values * cosine + rotate_half(values) * sine

def rms_norm(values, gain):
    return values * lax.rsqrt(lax.optimization_barrier(jnp.mean(values * values, axis=-1, keepdims=True)) + EPS) * gain

def layer(values, norm_attn, qkv_weight, qkv_bias, out_weight, norm_mlp, gate_up_weight, down_weight, allowed, cosine, sine):
    high = lax.Precision.HIGHEST
    count = values.shape[0]
    normed = low(rms_norm(values, norm_attn))
    qkv = low_back(jnp.dot(normed, qkv_weight, precision=high) + qkv_bias.reshape(-1))
    qkv = qkv.reshape(count, KV_HEADS, QKV_COLS)
    qcols = GROUP_Q * HEAD
    query = qkv[:, :, :qcols].reshape(count, KV_HEADS, GROUP_Q, HEAD)
    key = qkv[:, :, qcols:qcols + HEAD]
    value = qkv[:, :, qcols + HEAD:]
    query = low(rope_apply(query, cosine[:, None, None, :], sine[:, None, None, :]))
    key = low(rope_apply(key, cosine[:, None, :], sine[:, None, :]))
    value = low(value)
    factor = HEAD ** (-0.5)

    def one_group(item):
        group_query, group_key, group_value = item
        scores = low_back(jnp.einsum('thd,sd->hts', group_query, group_key, precision=high) * factor)
        scores = jnp.where(allowed[None], scores, -1e+30)
        probs = low(jax.nn.softmax(scores, axis=-1))
        return low(low_back(jnp.einsum('hts,sd->thd', probs, group_value, precision=high)))
    attended = lax.map(jax.checkpoint(one_group), (jnp.moveaxis(query, 1, 0), jnp.moveaxis(key, 1, 0), jnp.moveaxis(value, 1, 0)))
    attended = jnp.moveaxis(attended, 0, 1).reshape(count, KV_HEADS * GROUP_Q * HEAD)
    middle = values + low_back(jnp.dot(attended, out_weight, precision=high))
    normed2 = low(rms_norm(middle, norm_mlp))
    gate_up = low_back(jnp.einsum('td,dgf->tgf', normed2, gate_up_weight, precision=high))
    hidden = low(jax.nn.silu(gate_up[:, 0]) * gate_up[:, 1])
    return middle + low_back(jnp.dot(hidden, down_weight, precision=high))

def reference(tokens, cotangent, norm_attn, qkv_weight, qkv_bias, out_weight, norm_mlp, gate_up_weight, down_weight, lengths, deal):
    weights = tuple((w.astype(jnp.float32) for w in (norm_attn, qkv_weight, qkv_bias, out_weight, norm_mlp, gate_up_weight, down_weight)))

    def step(carry, item):
        pack_rows, pack_grad, seq_lengths, places = item
        segment, offset = segment_of(places, seq_lengths)
        cosine, sine = rotary(offset, HEAD)
        allowed = (segment[:, None] == segment[None, :]) & (places[None, :] <= places[:, None])

        def forward(values, *params):
            return layer(values, *params, allowed, cosine, sine)
        result, pullback = jax.vjp(forward, pack_rows, *weights)
        grads = pullback(pack_grad)
        carry = tuple((total + part for total, part in zip(carry, grads[1:])))
        return (carry, (result, grads[0]))
    zeros = tuple((jnp.zeros(w.shape, jnp.float32) for w in weights))
    items = (tokens.reshape(GROUPS, PACK, D), cotangent.reshape(GROUPS, PACK, D), lengths.astype(jnp.int32), deal.astype(jnp.int32))
    totals, (results, input_grads) = lax.scan(step, zeros, items)
    split_at = (GROUP_Q + 1) * HEAD
    return (results.reshape(TOKENS, D), input_grads.reshape(TOKENS, D), totals[0], totals[1], totals[2][:, :split_at], totals[2][:, split_at:], totals[3], totals[4], totals[5], totals[6])
```

```python
import jax
import jax.numpy as jnp
from jax import lax
from jax.sharding import PartitionSpec as P

HEAD = 128
GROUP_Q = 6
EPS = 1e-06
THETA = 1000000.0

bf16 = jnp.bfloat16
f32 = jnp.float32

TP_SWAP = [(0, 1), (1, 0)]
BLOCK = 128


def contract(left, right, left_dim, right_dim):
    return lax.dot_general(
        left, right, (((left_dim,), (right_dim,)), ((), ())), preferred_element_type=f32
    )


def after(value, *others):
    return lax.optimization_barrier((value,) + others)[0]


def gather(own, axis):
    copies = jnp.broadcast_to(own[None], (8,) + own.shape)
    return lax.all_to_all(copies, axis, 0, 0, tiled=True)


def reduce(part, axis):
    return jnp.sum(lax.all_to_all(part, axis, 0, 0, tiled=True).astype(f32), axis=0)


def gather_rows(own):
    mine = gather(own, "ctx").reshape(-1, own.shape[1])
    other = lax.ppermute(mine, "tp", TP_SWAP)
    return jnp.concatenate([mine, other], axis=0)


def reduce_rows(part):
    rows, width = part.shape
    part = part.astype(bf16)
    half = rows // 2
    got = lax.ppermute(part[half:], "tp", TP_SWAP)
    both = (part[:half].astype(f32) + got.astype(f32)).astype(bf16)
    return reduce(both.reshape(8, -1, width), "ctx")


def both_halves(own):
    t = lax.axis_index("tp")
    other = lax.ppermute(own, "tp", TP_SWAP)
    first = jnp.where(t == 0, own, other)
    second = jnp.where(t == 0, other, own)
    return jnp.concatenate([first, second], axis=0)


def segment_of(places, seq_lengths):
    ends = jnp.cumsum(seq_lengths)
    starts = ends - seq_lengths
    inside = ((places[:, None] >= starts[None, :]) & (places[:, None] < ends[None, :])).astype(
        jnp.int32
    )
    segment = jnp.sum(inside * jnp.arange(seq_lengths.shape[0], dtype=jnp.int32)[None, :], axis=1)
    offset = places - jnp.sum(inside * starts[None, :], axis=1)
    return (segment, offset)


def rotary(offset, width):
    half = width // 2
    freqs = THETA ** (-(2.0 * jnp.arange(half, dtype=f32)) / width)
    angle = offset.astype(f32)[:, None] * freqs[None, :]
    cosine = jnp.concatenate([jnp.cos(angle), jnp.cos(angle)], axis=1)
    sine = jnp.concatenate([jnp.sin(angle), jnp.sin(angle)], axis=1)
    return (cosine, sine)


def rope_apply(values, cosine, sine):
    half = values.shape[-1] // 2
    turned = jnp.concatenate([-values[..., half:], values[..., :half]], axis=-1)
    return values * cosine + turned * sine


def rope_back(grads, cosine, sine):
    half = grads.shape[-1] // 2
    scaled = grads * sine
    turned = jnp.concatenate([scaled[..., half:], -scaled[..., :half]], axis=-1)
    return grads * cosine + turned


def rms_scale(values):
    return lax.rsqrt(jnp.mean(values * values, axis=-1, keepdims=True) + EPS)


def norm_back(values, scale, gain, incoming):
    weighted = incoming * gain
    return scale * weighted - values * scale**3 * jnp.mean(
        weighted * values, axis=-1, keepdims=True
    )


def on_device(
    tokens,
    cotangent,
    norm_attn,
    qkv_weight,
    qkv_bias,
    out_weight,
    norm_mlp,
    gate_up_weight,
    down_weight,
    lengths,
    deal,
):
    f = lax.axis_index("fsdp")
    c = lax.axis_index("ctx")
    t = lax.axis_index("tp")
    count, width = tokens.shape
    own = count // 2
    shard = qkv_weight.shape[0]
    qcols = GROUP_Q * HEAD
    factor = HEAD ** (-0.5)
    has_head = c < GROUP_Q
    head = jnp.minimum(c, GROUP_Q - 1)

    tok = lax.dynamic_slice_in_dim(tokens, t * own, own)
    cot = lax.dynamic_slice_in_dim(cotangent, t * own, own)
    scale_a = rms_scale(tok)
    unit_own = (tok * scale_a).astype(bf16)
    grad_own = cot.astype(bf16)

    w_out_own = lax.dynamic_slice_in_dim(out_weight, head * HEAD, HEAD).T
    w_out_own = jnp.where(has_head, w_out_own, jnp.zeros_like(w_out_own))
    att_own = jnp.concatenate(
        [
            lax.dynamic_slice_in_dim(qkv_weight, head * HEAD, HEAD, axis=1),
            qkv_weight[:, qcols:],
            w_out_own,
        ],
        axis=1,
    )
    row = jnp.concatenate([norm_attn, norm_mlp, qkv_bias[0]])[None]
    att_own = jnp.concatenate([att_own, row, jnp.zeros((15, row.shape[1]), bf16)], axis=0)
    att_all = gather(att_own, "fsdp")
    w_att = att_all[:, :shard].reshape(width, -1)
    w_qkv = w_att[:, : 3 * HEAD]
    w_out = w_att[:, 3 * HEAD :]
    extra = att_all[:, shard].astype(f32)
    gain_a = extra[:, :shard].reshape(width)
    gain_m = extra[:, shard : 2 * shard].reshape(width)
    bias_all = extra[:, 2 * shard :].reshape(-1)
    bias = jnp.concatenate([lax.dynamic_slice_in_dim(bias_all, head * HEAD, HEAD), bias_all[qcols:]])

    start = jnp.maximum(4 * c, 5 * c - 5) * BLOCK
    units = 5 * BLOCK
    gu_own = lax.dynamic_slice_in_dim(gate_up_weight, start, units, axis=2)
    inside = (jnp.arange(units) < 4 * BLOCK) | (c >= 5)
    gu_own = jnp.where(inside, gu_own, jnp.zeros_like(gu_own))
    down_own = lax.dynamic_slice_in_dim(down_weight, start, units).T
    w_ffn = lax.all_gather(
        jnp.concatenate([gu_own[:, 0], gu_own[:, 1], down_own], axis=1), "fsdp", axis=0, tiled=True
    )
    w_gu = w_ffn[:, : 2 * units]
    w_down = w_ffn[:, 2 * units :]

    deal_all = deal[0].reshape(8, 2, own)[:, t ^ jnp.arange(2)]
    places = jnp.transpose(deal_all, (1, 0, 2)).reshape(-1)
    segment, offset = segment_of(places, lengths[0])
    cosine, sine = rotary(offset, HEAD)
    allowed = (segment[:, None] == segment[None, :]) & (places[None, :] <= places[:, None])

    unit_all = gather_rows(unit_own)
    normed = (unit_all.astype(f32) * gain_a).astype(bf16)
    grad_all = gather_rows(after(grad_own, unit_all))
    qkv = contract(normed, w_qkv, 1, 0) + bias
    query = rope_apply(qkv[:, :HEAD], cosine, sine).astype(bf16)
    key = rope_apply(qkv[:, HEAD : 2 * HEAD], cosine, sine).astype(bf16)
    value = qkv[:, 2 * HEAD :].astype(bf16)
    scores = jnp.where(allowed, contract(query, key, 1, 1) * factor, -1e30)
    raised = jnp.exp(scores - jnp.max(scores, axis=-1, keepdims=True))
    probs = raised / jnp.sum(raised, axis=-1, keepdims=True)
    probs_low = probs.astype(bf16)
    attended = contract(probs_low, value, 1, 0).astype(bf16)
    branch = reduce_rows(contract(attended, w_out, 1, 1))
    middle = tok + branch
    scale_m = rms_scale(middle)
    normed2 = gather_rows((middle * scale_m * gain_m).astype(bf16))

    gate_up = contract(normed2, w_gu, 1, 0)
    gate, upward = gate_up[:, :units], gate_up[:, units:]
    sigmoid = jax.nn.sigmoid(gate)
    activated = gate * sigmoid
    hidden = (activated * upward).astype(bf16)
    grad_hidden = contract(grad_all, w_down, 1, 0)
    grad_gate = grad_hidden * upward * sigmoid * (1.0 + gate * (1.0 - sigmoid))
    grad_up = grad_hidden * activated
    grad_gu = jnp.concatenate([grad_gate, grad_up], axis=1).astype(bf16)
    grad_normed2 = reduce_rows(contract(grad_gu, w_gu, 1, 1))
    mlp = reduce_rows(contract(hidden, w_down, 1, 1))
    output = both_halves(middle + mlp)

    def share(grad):
        mine = lax.psum_scatter(grad.astype(bf16), "fsdp", scatter_dimension=0, tiled=True)
        return gather(mine, "ctx")

    down_part = share(contract(grad_all, hidden, 0, 0))
    gu_part = share(contract(normed2, grad_gu, 0, 0))

    grad_middle = cot + norm_back(middle, scale_m, gain_m, grad_normed2)
    grad_branch = gather_rows(grad_middle.astype(bf16))
    grad_att = contract(grad_branch, w_out, 1, 0).astype(bf16)
    grad_probs = contract(grad_att, value, 1, 1)
    grad_value = contract(probs_low, grad_att, 0, 0)
    grad_scores = (
        probs * (grad_probs - jnp.sum(probs * grad_probs, axis=-1, keepdims=True))
    ).astype(bf16)
    grad_query = contract(grad_scores, key, 1, 0) * factor
    grad_key = contract(grad_scores, query, 0, 0) * factor
    grad_qkv = jnp.concatenate(
        [rope_back(grad_query, cosine, sine), rope_back(grad_key, cosine, sine), grad_value],
        axis=1,
    ).astype(bf16)
    grad_normed = reduce_rows(contract(grad_qkv, w_qkv, 1, 1))
    grad_tokens = both_halves(grad_middle + norm_back(tok, scale_a, gain_a, grad_normed))

    att_grads = jnp.concatenate(
        [contract(normed, grad_qkv, 0, 0), contract(grad_branch, attended, 0, 0)], axis=1
    ).reshape(8, shard, 4 * HEAD)
    sums = jnp.sum(grad_qkv.astype(f32), axis=0)
    sums = jnp.concatenate([sums, jnp.zeros((HEAD,), f32)])
    sums = jnp.broadcast_to(sums, (8, 1, 4 * HEAD))
    pad = jnp.zeros((8, 15, 4 * HEAD), f32)
    att_part = reduce(jnp.concatenate([att_grads, sums, pad], axis=1).astype(bf16), "fsdp")
    att_part = gather(att_part.astype(bf16), "ctx").astype(f32)
    heads = att_part[:GROUP_Q]
    kv_sum = jnp.sum(heads[:, : shard + 1, HEAD : 3 * HEAD], axis=0)
    q_cols = jnp.transpose(heads[:, : shard + 1, :HEAD], (1, 0, 2)).reshape(shard + 1, qcols)
    all_cols = jnp.concatenate([q_cols, kv_sum], axis=1)
    grad_qkv_weight = all_cols[:shard]
    bias_grad = all_cols[shard]
    split_at = qcols + HEAD
    own_bias = lax.dynamic_slice_in_dim(bias_grad, f * (split_at // 8), split_at // 8)[None]
    own_value = lax.dynamic_slice_in_dim(bias_grad, split_at + f * (HEAD // 8), HEAD // 8)[None]
    grad_out_weight = jnp.transpose(heads[:, :shard, 3 * HEAD :], (0, 2, 1)).reshape(qcols, shard)

    def joined(parts):
        return jnp.concatenate(
            [parts[i, :, : (4 if i < 5 else 5) * BLOCK] for i in range(8)], axis=1
        ).astype(f32)

    grad_gu_weight = jnp.stack([joined(gu_part[..., :units]), joined(gu_part[..., units:])], axis=1)
    grad_down_weight = joined(down_part).T

    gain_sums = jnp.stack(
        [
            jnp.sum(grad_qkv_weight * qkv_weight.astype(f32), axis=1) / norm_attn.astype(f32),
            jnp.sum(grad_gu_weight * gate_up_weight.astype(f32), axis=(1, 2))
            / norm_mlp.astype(f32),
        ]
    )
    gain_sums = gain_sums + lax.ppermute(gain_sums, "tp", TP_SWAP)

    return (
        output,
        grad_tokens,
        gain_sums[0],
        grad_qkv_weight,
        own_bias,
        own_value,
        grad_out_weight,
        gain_sums[1],
        grad_gu_weight,
        grad_down_weight,
    )


def solution(mesh):
    in_specs = (
        P(("fsdp", "ctx"), None),
        P(("fsdp", "ctx"), None),
        P("fsdp"),
        P("fsdp", "tp"),
        P("tp", "fsdp"),
        P("tp", "fsdp"),
        P("fsdp"),
        P("fsdp", None, "tp"),
        P("tp", "fsdp"),
        P("fsdp", None),
        P("fsdp", None),
    )
    out_specs = (
        P(("fsdp", "ctx"), None),
        P(("fsdp", "ctx"), None),
        P("fsdp"),
        P("fsdp", "tp"),
        P("tp", "fsdp"),
        P("tp", "fsdp"),
        P("tp", "fsdp"),
        P("fsdp"),
        P("fsdp", None, "tp"),
        P("tp", "fsdp"),
    )
    return jax.shard_map(
        on_device, mesh=mesh, in_specs=in_specs, out_specs=out_specs, check_vma=False
    )
```

```python
import jax
import jax.numpy as jnp
from jax import lax
from jax.experimental import pallas as pl
from jax.experimental.pallas import tpu as pltpu
from jax.sharding import PartitionSpec as P

HEAD = 128
GROUP_Q = 6
EPS = 1e-06
THETA = 1000000.0

bf16 = jnp.bfloat16
f32 = jnp.float32

BLOCK = 128
ROWS = 256
GRAD_ROWS = 64
VMEM_BYTES = 60 * 2**20
COST = pl.CostEstimate(flops=10**6, bytes_accessed=10**5, transcendentals=0)

TP_SWAP = [(0, 1), (1, 0)]
XH_SWAP = [(i, i ^ 4) for i in range(8)]
XL_SWAP = [(i, i ^ 1) for i in range(8)]
Y_GROUPS = [[0, 1, 2, 3], [4, 5, 6, 7]]
Z_GROUPS = [[0, 2, 4, 6], [1, 3, 5, 7]]


def y_shift(k):
    return [(h * 4 + y, h * 4 + (y + k) % 4) for h in range(2) for y in range(4)]


def contract(left, right, left_dim, right_dim):
    return lax.dot_general(
        left, right, (((left_dim,), (right_dim,)), ((), ())), preferred_element_type=f32
    )


def tie(*values):
    return lax.optimization_barrier(values)


def ordered(own, other, place):
    return jnp.stack([jnp.where(place == 0, own, other), jnp.where(place == 0, other, own)])


def gather(own, axis):
    copies = jnp.broadcast_to(own[None], (8,) + own.shape)
    return lax.all_to_all(copies, axis, 0, 0, tiled=True)


def reduce(part, axis):
    return jnp.sum(lax.all_to_all(part, axis, 0, 0, tiled=True).astype(f32), axis=0)


def gather_small(own, far):
    me = lax.axis_index("fsdp")
    hi, y = me // 4, me % 4
    out = jnp.zeros((8,) + own.shape, own.dtype)
    for d, base in ((0, own), (1, far)):
        out = lax.dynamic_update_index_in_dim(out, base, (hi ^ d) * 4 + y, 0)
        for k in (1, 3, 2):
            piece = lax.ppermute(base, "fsdp", y_shift(k))
            out = lax.dynamic_update_index_in_dim(out, piece, (hi ^ d) * 4 + (y - k + 4) % 4, 0)
    return out


def gather_along_y(own):
    return lax.all_gather(own, "fsdp", axis=0, axis_index_groups=Y_GROUPS, tiled=True)


def by_y(part):
    rows, width = part.shape
    return jnp.swapaxes(part.astype(bf16).reshape(2, 4, -1, width), 0, 1).reshape(rows, width)


def reduce_along_y(part):
    pair = lax.psum_scatter(
        part, "fsdp", scatter_dimension=0, axis_index_groups=Y_GROUPS, tiled=True
    )
    return pair.reshape(2, -1, part.shape[1])


def reduce_over_hi(pair):
    hi = lax.axis_index("fsdp") // 4
    kept = jnp.where(hi == 0, pair[0], pair[1])
    sent = jnp.where(hi == 0, pair[1], pair[0])
    return (kept.astype(f32) + lax.ppermute(sent, "fsdp", XH_SWAP).astype(f32)).astype(bf16)


def gather_along_z(own):
    return lax.all_gather(own, "ctx", axis=0, axis_index_groups=Z_GROUPS)


def reduce_along_z(part):
    pair = lax.psum_scatter(
        part, "ctx", scatter_dimension=0, axis_index_groups=Z_GROUPS, tiled=True
    )
    return pair.reshape(2, -1, part.shape[1])


def reduce_over_lo(pair):
    lo = lax.axis_index("ctx") % 2
    kept = jnp.where(lo == 0, pair[0], pair[1])
    sent = jnp.where(lo == 0, pair[1], pair[0])
    return kept.astype(f32) + lax.ppermute(sent, "ctx", XL_SWAP).astype(f32)


def gather_over_lo(own):
    return ordered(own, lax.ppermute(own, "ctx", XL_SWAP), lax.axis_index("ctx") % 2)


def both_cores(mine):
    mine = mine.reshape(-1, mine.shape[-1])
    return [mine, lax.ppermute(mine, "tp", TP_SWAP)]


def pair_sums(mine, other):
    got = lax.ppermute(other, "tp", TP_SWAP)
    total = (mine.astype(f32) + got.astype(f32)).astype(bf16)
    return total.reshape(8, -1, total.shape[1])


def over_rows(lefts, rights):
    return contract(lefts[0], rights[0], 0, 0) + contract(lefts[1], rights[1], 0, 0)


def both_halves(own):
    t = lax.axis_index("tp")
    other = lax.ppermute(own, "tp", TP_SWAP)
    first = jnp.where(t == 0, own, other)
    second = jnp.where(t == 0, other, own)
    return jnp.concatenate([first, second], axis=0)


def rope_in(values, cosine, sine):
    return values * cosine + pltpu.roll(values, HEAD // 2, 1) * sine


def rope_out(grads, cosine, sine):
    return grads * cosine - pltpu.roll(grads, HEAD // 2, 1) * sine


def masked_scores(query, key, first, last, places):
    scores = contract(query, key, 1, 1) * HEAD ** (-0.5)
    return jnp.where((places >= first) & (places <= last), scores, -1e30)


def attention_kernel(
    mine, other, gain, att, bias, cosine, sine, first, last, places,
    query, key, value, attended, log_total, branch_mine, branch_other, weight,
):
    shard = weight.shape[0] // 8
    for i in range(8):
        weight[i * shard : (i + 1) * shard, :] = att[i, :shard, :]
    for i in range(4):
        at = slice(i * ROWS, (i + 1) * ROWS)
        half = slice(i % 2 * ROWS, (i % 2 + 1) * ROWS)
        rows = (mine if i < 2 else other)[half, :]
        normed = (rows.astype(f32) * gain[...]).astype(bf16)
        qkv = contract(normed, weight[:, : 3 * HEAD], 1, 0) + bias[...]
        query[at, :] = rope_in(qkv[:, :HEAD], cosine[at, :], sine[at, :]).astype(bf16)
        key[at, :] = rope_in(qkv[:, HEAD : 2 * HEAD], cosine[at, :], sine[at, :]).astype(bf16)
        value[at, :] = qkv[:, 2 * HEAD :].astype(bf16)
    for i in range(4):
        at = slice(i * ROWS, (i + 1) * ROWS)
        half = slice(i % 2 * ROWS, (i % 2 + 1) * ROWS)
        scores = masked_scores(query[at, :], key[...], first[at, :], last[at, :], places[...])
        top = jnp.max(scores, axis=1, keepdims=True)
        raised = jnp.exp(scores - top)
        total = jnp.sum(raised, axis=1, keepdims=True)
        log_total[at, :] = top + jnp.log(total)
        probs = (raised / total).astype(bf16)
        rows = contract(probs, value[...], 1, 0).astype(bf16)
        attended[at, :] = rows
        branch = contract(rows, weight[:, 3 * HEAD :], 1, 1).astype(bf16)
        (branch_mine if i < 2 else branch_other)[half, :] = branch


def attention_grad_kernel(
    branch_mine, branch_other, mine, other, gain, att, query, key, value, attended, log_total,
    cosine, sine, first, last, places,
    normed_mine, normed_other, grads, weight, normed, grad_qkv, grad_key, grad_value,
):
    shard = weight.shape[0] // 8
    for i in range(8):
        weight[i * shard : (i + 1) * shard, :] = att[i, :shard, :]
    for i in range(4):
        at = slice(i * ROWS, (i + 1) * ROWS)
        half = slice(i % 2 * ROWS, (i % 2 + 1) * ROWS)
        rows = (mine if i < 2 else other)[half, :]
        normed[at, :] = (rows.astype(f32) * gain[...]).astype(bf16)
        branch = (branch_mine if i < 2 else branch_other)[half, :]
        grad_att = contract(branch, weight[:, 3 * HEAD :], 1, 0).astype(bf16)
        scores = masked_scores(query[at, :], key[...], first[at, :], last[at, :], places[...])
        probs = jnp.exp(scores - log_total[at, :])
        grad_probs = contract(grad_att, value[...], 1, 1)
        inner = jnp.sum(probs * grad_probs, axis=1, keepdims=True)
        grad_scores = (probs * (grad_probs - inner)).astype(bf16)
        grad_query = contract(grad_scores, key[...], 1, 0) * HEAD ** (-0.5)
        grad_qkv[at, :HEAD] = rope_out(grad_query, cosine[at, :], sine[at, :]).astype(bf16)
        key_part = contract(grad_scores, query[at, :], 0, 0)
        value_part = contract(probs.astype(bf16), grad_att, 0, 0)
        if i == 0:
            grad_key[...] = key_part
            grad_value[...] = value_part
        else:
            grad_key[...] += key_part
            grad_value[...] += value_part
    grad_key_pre = rope_out(grad_key[...] * HEAD ** (-0.5), cosine[...], sine[...])
    grad_qkv[:, HEAD : 2 * HEAD] = grad_key_pre.astype(bf16)
    grad_qkv[:, 2 * HEAD :] = grad_value[...].astype(bf16)
    for i in range(4):
        at = slice(i * ROWS, (i + 1) * ROWS)
        half = slice(i % 2 * ROWS, (i % 2 + 1) * ROWS)
        rows = contract(grad_qkv[at, :], weight[:, : 3 * HEAD], 1, 1).astype(bf16)
        (normed_mine if i < 2 else normed_other)[half, :] = rows
    sums = jnp.sum(grad_qkv[...].astype(f32), axis=0, keepdims=True)
    sums = jnp.concatenate([sums, jnp.zeros((1, HEAD), f32)], axis=1)
    pad = jnp.where(lax.broadcasted_iota(jnp.int32, (16, 4 * HEAD), 0) == 0, sums, 0.0).astype(bf16)
    top = attended[: 2 * ROWS, :]
    low = attended[2 * ROWS :, :]
    for i in range(4):
        cols = slice(2 * i * shard, 2 * (i + 1) * shard)
        qkv_part = contract(normed[:, cols], grad_qkv[...], 0, 0)
        out_part = contract(branch_mine[:, cols], top, 0, 0)
        out_part += contract(branch_other[:, cols], low, 0, 0)
        both = jnp.concatenate([qkv_part, out_part], axis=1).astype(bf16)
        for j in range(2):
            place = (2 * i + j) % 4 * 2 + (2 * i + j) // 4
            base = place * (shard + 16)
            grads[base : base + shard, :] = both[j * shard : (j + 1) * shard, :]
            grads[base + shard : base + shard + 16, :] = pad


def ffn_kernel(hi, rows, grad, weight_own, weight_far, hidden, grad_gu, grad_rows):
    width = weight_own.shape[0]
    units = weight_own.shape[1] // 3
    at_own = pl.ds(pl.multiple_of(hi[0] * width, HEAD), width)
    at_far = pl.ds(pl.multiple_of((1 - hi[0]) * width, HEAD), width)

    def product(left, cols):
        return contract(left[:, at_own], weight_own[:, cols], 1, 0) + contract(
            left[:, at_far], weight_far[:, cols], 1, 0
        )

    gate = product(rows, slice(0, units))
    upward = product(rows, slice(units, 2 * units))
    sigmoid = jax.nn.sigmoid(gate)
    activated = gate * sigmoid
    hidden[...] = (activated * upward).astype(bf16)
    grad_hidden = product(grad, slice(2 * units, 3 * units))
    grad_gu[:, :units] = (
        grad_hidden * upward * sigmoid * (1.0 + gate * (1.0 - sigmoid))
    ).astype(bf16)
    grad_gu[:, units:] = (grad_hidden * activated).astype(bf16)
    for at, weight in ((at_own, weight_own), (at_far, weight_far)):
        grad_rows[:, at] = contract(grad_gu[...], weight[:, : 2 * units], 1, 1).astype(bf16)


def down_grad_kernel(parts, out):
    start = 0
    for i in range(8):
        cols = (4 if i < 5 else 5) * BLOCK
        out[:, start : start + cols] = parts[i, :, :cols].astype(f32)
        start += cols


def gate_up_grad_kernel(parts, out):
    units = parts.shape[2] // 2
    start = 0
    for i in range(8):
        for j in range(4 if i < 5 else 5):
            for k in range(2):
                cols = slice(k * units + j * BLOCK, k * units + (j + 1) * BLOCK)
                out[:, k, start : start + BLOCK] = parts[i, :, cols].astype(f32)
            start += BLOCK


def attention_weight_grad_kernel(parts, grad_qkv, grad_out, sums):
    shard = grad_qkv.shape[0]
    qcols = GROUP_Q * HEAD
    pairs = 0.0
    tails = 0.0
    for i in range(GROUP_Q):
        cols = slice(i * HEAD, (i + 1) * HEAD)
        grad_qkv[:, cols] = parts[i, :shard, :HEAD].astype(f32)
        grad_out[:, cols] = parts[i, :shard, 3 * HEAD :].astype(f32)
        tail = parts[i, shard:, :].astype(f32)
        sums[:, cols] = tail[:, :HEAD]
        pairs += parts[i, :shard, HEAD : 3 * HEAD].astype(f32)
        tails += tail[:, HEAD : 3 * HEAD]
    grad_qkv[:, qcols:] = pairs
    sums[:, qcols:] = tails


def local_call(kernel, outs, scratch=()):
    return pl.pallas_call(
        kernel,
        out_shape=[jax.ShapeDtypeStruct(shape, dtype) for shape, dtype in outs],
        scratch_shapes=[pltpu.VMEM(shape, dtype) for shape, dtype in scratch],
        compiler_params=pltpu.CompilerParams(vmem_limit_bytes=VMEM_BYTES),
        cost_estimate=COST,
    )


def assemble(kernel, parts, outs):
    return local_call(kernel, outs)(parts)


def attention(mine, other, gain, att, bias, cosine, sine, first, last, places):
    half, width = mine.shape
    outs = [((2 * half, HEAD), bf16)] * 4 + [((2 * half, 1), f32)] + [((half, width), bf16)] * 2
    return local_call(attention_kernel, outs, [((width, 4 * HEAD), bf16)])(
        mine, other, gain, att, bias, cosine, sine, first, last, places
    )


def attention_grad(branch_mine, branch_other, mine, other, gain, att, *rest):
    half, width = mine.shape
    outs = [((half, width), bf16)] * 2 + [((width + 8 * 16, 4 * HEAD), bf16)]
    scratch = [
        ((width, 4 * HEAD), bf16),
        ((2 * half, width), bf16),
        ((2 * half, 3 * HEAD), bf16),
        ((2 * half, HEAD), f32),
        ((2 * half, HEAD), f32),
    ]
    return local_call(attention_grad_kernel, outs, scratch)(
        branch_mine, branch_other, mine, other, gain, att, *rest
    )


def feed_forward(hi, rows, grad, weight_own, weight_far):
    count, width = rows.shape
    units = weight_own.shape[1] // 3

    def by_rows(cols):
        return pl.BlockSpec((ROWS, cols), lambda i, hi: (i, 0))

    whole = pl.BlockSpec(weight_own.shape, lambda i, hi: (0, 0))
    return pl.pallas_call(
        ffn_kernel,
        grid_spec=pltpu.PrefetchScalarGridSpec(
            num_scalar_prefetch=1,
            grid=(count // ROWS,),
            in_specs=[by_rows(width), by_rows(width), whole, whole],
            out_specs=[by_rows(units), by_rows(2 * units), by_rows(width)],
        ),
        out_shape=[
            jax.ShapeDtypeStruct((count, cols), bf16) for cols in (units, 2 * units, width)
        ],
        compiler_params=pltpu.CompilerParams(vmem_limit_bytes=VMEM_BYTES),
        cost_estimate=COST,
    )(hi, rows, grad, weight_own, weight_far)


def sequence_of(places, seq_lengths):
    ends = jnp.cumsum(seq_lengths)
    starts = ends - seq_lengths
    inside = (places[:, None] >= starts[None, :]) & (places[:, None] < ends[None, :])
    return jnp.sum(inside.astype(jnp.int32) * starts[None, :], axis=1)


def rotary(offset):
    half = HEAD // 2
    freqs = THETA ** (-(2.0 * jnp.arange(half, dtype=f32)) / HEAD)
    angle = offset.astype(f32)[:, None] * freqs[None, :]
    cosine, sine = jnp.cos(angle), jnp.sin(angle)
    return jnp.concatenate([cosine, cosine], axis=1), jnp.concatenate([-sine, sine], axis=1)


def rms_scale(values):
    return lax.rsqrt(jnp.mean(values * values, axis=-1, keepdims=True) + EPS)


def norm_back(values, scale, gain, incoming):
    weighted = incoming * gain
    return scale * weighted - values * scale**3 * jnp.mean(
        weighted * values, axis=-1, keepdims=True
    )


def on_device(
    tokens,
    cotangent,
    norm_attn,
    qkv_weight,
    qkv_bias,
    out_weight,
    norm_mlp,
    gate_up_weight,
    down_weight,
    lengths,
    deal,
):
    f = lax.axis_index("fsdp")
    c = lax.axis_index("ctx")
    t = lax.axis_index("tp")
    count, width = tokens.shape
    own = count // 2
    shard = qkv_weight.shape[0]
    qcols = GROUP_Q * HEAD
    has_head = c < GROUP_Q
    head = jnp.minimum(c, GROUP_Q - 1)

    tok = lax.dynamic_slice_in_dim(tokens, t * own, own)
    cot = lax.dynamic_slice_in_dim(cotangent, t * own, own)
    scale_a = rms_scale(tok)
    unit_own = (tok * scale_a).astype(bf16)
    grad_own = cot.astype(bf16)

    w_out_own = lax.dynamic_slice_in_dim(out_weight, head * HEAD, HEAD).T
    w_out_own = jnp.where(has_head, w_out_own, jnp.zeros_like(w_out_own))
    att_own = jnp.concatenate(
        [
            lax.dynamic_slice_in_dim(qkv_weight, head * HEAD, HEAD, axis=1),
            qkv_weight[:, qcols:],
            w_out_own,
        ],
        axis=1,
    )
    row = jnp.concatenate([norm_attn, norm_mlp, qkv_bias[0]])[None]
    att_own = jnp.concatenate([att_own, row, jnp.zeros((15, row.shape[1]), bf16)], axis=0)
    att_far = lax.ppermute(att_own, "fsdp", XH_SWAP)

    start = jnp.maximum(4 * c, 5 * c - 5) * BLOCK
    units = 5 * BLOCK
    gu_own = lax.dynamic_slice_in_dim(gate_up_weight, start, units, axis=2)
    inside = (jnp.arange(units) < 4 * BLOCK) | (c >= 5)
    gu_own = jnp.where(inside, gu_own, jnp.zeros_like(gu_own))
    down_own = lax.dynamic_slice_in_dim(down_weight, start, units).T
    ffn_own = jnp.concatenate([gu_own[:, 0], gu_own[:, 1], down_own], axis=1)
    ffn_line = gather_along_y(ffn_own)
    ffn_far = lax.ppermute(ffn_own, "fsdp", XH_SWAP)

    att_all = gather_small(att_own, att_far)
    extra = att_all[:, shard].astype(f32)
    gain_a = extra[:, :shard].reshape(1, width)
    gain_m = extra[:, shard : 2 * shard].reshape(1, width)
    bias_all = extra[:, 2 * shard :].reshape(1, -1)
    bias = jnp.concatenate(
        [lax.dynamic_slice_in_dim(bias_all, head * HEAD, HEAD, axis=1), bias_all[:, qcols:]], axis=1
    )

    deal_all = deal[0].reshape(8, 2, own)[:, t ^ jnp.arange(2)]
    places = jnp.transpose(deal_all, (1, 0, 2)).reshape(-1)
    first = sequence_of(places, lengths[0])
    cosine, sine = rotary(places - first)
    order = (cosine, sine, first[:, None], places[:, None], places[None, :])

    unit_mine, grad_own = tie(gather(unit_own, "ctx"), grad_own)
    grad_mine = gather(grad_own, "ctx")
    units_all = both_cores(unit_mine)
    held = attention(*units_all, gain_a, att_all, bias, *order)
    *held, grad_mine, ffn_far = tie(*held, grad_mine, ffn_far)
    query, key, value, attended, log_total, branch_mine, branch_other = held
    ffn_far = gather_along_y(ffn_far)
    grads = both_cores(grad_mine)
    branch_parts = pair_sums(branch_mine, branch_other)
    branch = reduce(branch_parts, "ctx")
    middle = tok + branch
    scale_m = rms_scale(middle)
    normed2_mine = gather((middle * scale_m * gain_m).astype(bf16), "ctx")
    normed2 = both_cores(normed2_mine)

    hi = (f // 4)[None]
    hidden, grad_gu, parts = zip(
        *[feed_forward(hi, r, g, ffn_line, ffn_far) for r, g in zip(normed2, grads)]
    )
    parts = pair_sums(*parts)
    parts, *held = tie(parts, *normed2, *grad_gu, *hidden, *grads)
    normed2, grad_gu, hidden, grads = held[0:2], held[2:4], held[4:6], held[6:8]
    grad_normed2 = reduce(parts, "ctx")

    down_sums = reduce_along_y(by_y(over_rows(grads, hidden)))
    grad_normed2, gu_blocks = tie(grad_normed2, by_y(over_rows(normed2, grad_gu)))
    gu_sums = reduce_along_y(gu_blocks)

    def output_rows(rows):
        own_side = contract(rows, ffn_line[:, 2 * units :], 1, 1).astype(bf16)
        far_side = contract(rows, ffn_far[:, 2 * units :], 1, 1).astype(bf16)
        return jnp.concatenate(
            [jnp.where(f < 4, own_side, far_side), jnp.where(f < 4, far_side, own_side)], axis=1
        )

    grad_middle = cot + norm_back(middle, scale_m, gain_m, grad_normed2)
    branch_mine = gather(grad_middle.astype(bf16), "ctx")
    branch_mine, down_share = tie(branch_mine, reduce_over_hi(down_sums))
    grad_branch = both_cores(branch_mine)
    down_part = gather(down_share, "ctx")
    normed_mine, normed_other, att_grads = attention_grad(
        *grad_branch, *units_all, gain_a, att_all, query, key, value, attended, log_total, *order
    )
    att_grads, down_part = tie(att_grads, down_part)
    att_sums = reduce_along_y(att_grads)
    normed_parts = pair_sums(normed_mine, normed_other)
    grad_normed, gu_share, *hidden = tie(
        reduce(normed_parts, "ctx"), reduce_over_hi(gu_sums), *hidden
    )
    gu_part = gather(gu_share, "ctx")
    grad_tokens = both_halves(grad_middle + norm_back(tok, scale_a, gain_a, grad_normed))
    output_parts = pair_sums(*[output_rows(h) for h in hidden])
    grad_down_weight = assemble(
        down_grad_kernel, down_part, [((shard, down_weight.shape[0]), f32)]
    )[0]
    att_share, gu_part, output_parts, grad_down_weight, grad_tokens = tie(
        reduce_over_hi(att_sums), gu_part, output_parts, grad_down_weight, grad_tokens
    )
    att_part = gather(att_share, "ctx")
    output_pair = reduce_along_z(output_parts.reshape(-1, width))
    output = both_halves(middle + reduce_over_lo(output_pair))
    grad_gu_weight = pl.pallas_call(
        gate_up_grad_kernel,
        grid=(shard // GRAD_ROWS,),
        in_specs=[pl.BlockSpec((8, GRAD_ROWS, 2 * units), lambda i: (0, i, 0))],
        out_specs=pl.BlockSpec((GRAD_ROWS,) + gate_up_weight.shape[1:], lambda i: (i, 0, 0)),
        out_shape=jax.ShapeDtypeStruct(gate_up_weight.shape, f32),
        compiler_params=pltpu.CompilerParams(vmem_limit_bytes=VMEM_BYTES),
        cost_estimate=COST,
    )(gu_part)
    grad_qkv_weight, grad_out_weight, sums = assemble(
        attention_weight_grad_kernel,
        att_part,
        [(qkv_weight.shape, f32), ((shard, qcols), f32), ((16, qkv_weight.shape[1]), f32)],
    )
    split_at = qcols + HEAD
    own_bias = lax.dynamic_slice(sums, (0, f * (split_at // 8)), (1, split_at // 8))
    own_value = lax.dynamic_slice(sums, (0, split_at + f * (HEAD // 8)), (1, HEAD // 8))
    gain_sums = jnp.stack(
        [
            jnp.sum(grad_qkv_weight * qkv_weight.astype(f32), axis=1) / norm_attn.astype(f32),
            jnp.sum(grad_gu_weight * gate_up_weight.astype(f32), axis=(1, 2))
            / norm_mlp.astype(f32),
        ]
    )
    gain_sums = gain_sums + lax.ppermute(gain_sums, "tp", TP_SWAP)

    return (
        output,
        grad_tokens,
        gain_sums[0],
        grad_qkv_weight,
        own_bias,
        own_value,
        grad_out_weight.T,
        gain_sums[1],
        grad_gu_weight,
        grad_down_weight.T,
    )


def solution(mesh):
    in_specs = (
        P(("fsdp", "ctx"), None),
        P(("fsdp", "ctx"), None),
        P("fsdp"),
        P("fsdp", "tp"),
        P("tp", "fsdp"),
        P("tp", "fsdp"),
        P("fsdp"),
        P("fsdp", None, "tp"),
        P("tp", "fsdp"),
        P("fsdp", None),
        P("fsdp", None),
    )
    out_specs = (
        P(("fsdp", "ctx"), None),
        P(("fsdp", "ctx"), None),
        P("fsdp"),
        P("fsdp", "tp"),
        P("tp", "fsdp"),
        P("tp", "fsdp"),
        P("tp", "fsdp"),
        P("fsdp"),
        P("fsdp", None, "tp"),
        P("tp", "fsdp"),
    )
    return jax.shard_map(
        on_device, mesh=mesh, in_specs=in_specs, out_specs=out_specs, check_vma=False
    )
```

```python
import jax
import jax.numpy as jnp
from jax import lax
from jax.experimental import pallas as pl
from jax.experimental.pallas import tpu as pltpu
from jax.sharding import PartitionSpec as P

HEAD = 128
GROUP_Q = 6
EPS = 1e-06
THETA = 1000000.0

bf16 = jnp.bfloat16
f32 = jnp.float32

BLOCK = 128
ROWS = 256
GRAD_ROWS = 64
VMEM_BYTES = 60 * 2**20
COST = pl.CostEstimate(flops=10**6, bytes_accessed=10**5, transcendentals=0)

TP_SWAP = [(0, 1), (1, 0)]
XH_SWAP = [(i, i ^ 4) for i in range(8)]
XL_SWAP = [(i, i ^ 1) for i in range(8)]
Y_GROUPS = [[0, 1, 2, 3], [4, 5, 6, 7]]
Z_GROUPS = [[0, 2, 4, 6], [1, 3, 5, 7]]


def y_shift(k):
    return [(h * 4 + y, h * 4 + (y + k) % 4) for h in range(2) for y in range(4)]


def contract(left, right, left_dim, right_dim):
    return lax.dot_general(
        left, right, (((left_dim,), (right_dim,)), ((), ())), preferred_element_type=f32
    )


def tie(*values):
    return lax.optimization_barrier(values)


def ordered(own, other, place):
    return jnp.stack([jnp.where(place == 0, own, other), jnp.where(place == 0, other, own)])


def gather(own, axis):
    copies = jnp.broadcast_to(own[None], (8,) + own.shape)
    return lax.all_to_all(copies, axis, 0, 0, tiled=True)


def spread(part, axis):
    return lax.all_to_all(part, axis, 0, 0, tiled=True)


def summed(parts):
    return jnp.sum(parts.astype(f32), axis=0)


def gather_small(own, far):
    me = lax.axis_index("fsdp")
    hi, y = me // 4, me % 4
    out = jnp.zeros((8,) + own.shape, own.dtype)
    for d, base in ((0, own), (1, far)):
        out = lax.dynamic_update_index_in_dim(out, base, (hi ^ d) * 4 + y, 0)
        for k in (1, 3, 2):
            piece = lax.ppermute(base, "fsdp", y_shift(k))
            out = lax.dynamic_update_index_in_dim(out, piece, (hi ^ d) * 4 + (y - k + 4) % 4, 0)
    return out


def gather_along_y(own):
    return lax.all_gather(own, "fsdp", axis=0, axis_index_groups=Y_GROUPS, tiled=True)


def by_y(part):
    rows, width = part.shape
    return jnp.swapaxes(part.astype(bf16).reshape(2, 4, -1, width), 0, 1).reshape(rows, width)


def reduce_along_y(part):
    pair = lax.psum_scatter(
        part, "fsdp", scatter_dimension=0, axis_index_groups=Y_GROUPS, tiled=True
    )
    return pair.reshape(2, -1, part.shape[1])


def swap_over_hi(pair):
    hi = lax.axis_index("fsdp") // 4
    sent = jnp.where(hi == 0, pair[1], pair[0])
    return jnp.where(hi == 0, pair[0], pair[1]), lax.ppermute(sent, "fsdp", XH_SWAP)


def added(kept, got):
    return (kept.astype(f32) + got.astype(f32)).astype(bf16)


def gather_along_z(own):
    return lax.all_gather(own, "ctx", axis=0, axis_index_groups=Z_GROUPS)


def both_cores(mine):
    mine = mine.reshape(-1, mine.shape[-1])
    return [mine, lax.ppermute(mine, "tp", TP_SWAP)]


def pair_sums(mine, other):
    got = lax.ppermute(other, "tp", TP_SWAP)
    total = (mine.astype(f32) + got.astype(f32)).astype(bf16)
    return total.reshape(8, -1, total.shape[1])


def over_rows(lefts, rights):
    return contract(lefts[0], rights[0], 0, 0) + contract(lefts[1], rights[1], 0, 0)


def both_halves(own):
    t = lax.axis_index("tp")
    other = lax.ppermute(own, "tp", TP_SWAP)
    first = jnp.where(t == 0, own, other)
    second = jnp.where(t == 0, other, own)
    return jnp.concatenate([first, second], axis=0)


def rope_in(values, cosine, sine):
    return values * cosine + pltpu.roll(values, HEAD // 2, 1) * sine


def rope_out(grads, cosine, sine):
    return grads * cosine - pltpu.roll(grads, HEAD // 2, 1) * sine


def masked_scores(query, key, first, last, places):
    scores = contract(query, key, 1, 1) * HEAD ** (-0.5)
    return jnp.where((places >= first) & (places <= last), scores, -1e30)


def attention_kernel(
    mine, other, gain, att, bias, cosine, sine, first, last, places,
    query, key, value, attended, log_total, branch_mine, branch_other, weight,
):
    shard = weight.shape[0] // 8
    for i in range(8):
        weight[i * shard : (i + 1) * shard, :] = att[i, :shard, :]
    for i in range(4):
        at = slice(i * ROWS, (i + 1) * ROWS)
        half = slice(i % 2 * ROWS, (i % 2 + 1) * ROWS)
        rows = (mine if i < 2 else other)[half, :]
        normed = (rows.astype(f32) * gain[...]).astype(bf16)
        qkv = contract(normed, weight[:, : 3 * HEAD], 1, 0) + bias[...]
        query[at, :] = rope_in(qkv[:, :HEAD], cosine[at, :], sine[at, :]).astype(bf16)
        key[at, :] = rope_in(qkv[:, HEAD : 2 * HEAD], cosine[at, :], sine[at, :]).astype(bf16)
        value[at, :] = qkv[:, 2 * HEAD :].astype(bf16)
    for i in range(4):
        at = slice(i * ROWS, (i + 1) * ROWS)
        half = slice(i % 2 * ROWS, (i % 2 + 1) * ROWS)
        scores = masked_scores(query[at, :], key[...], first[at, :], last[at, :], places[...])
        top = jnp.max(scores, axis=1, keepdims=True)
        raised = jnp.exp(scores - top)
        total = jnp.sum(raised, axis=1, keepdims=True)
        log_total[at, :] = top + jnp.log(total)
        probs = (raised / total).astype(bf16)
        rows = contract(probs, value[...], 1, 0).astype(bf16)
        attended[at, :] = rows
        branch = contract(rows, weight[:, 3 * HEAD :], 1, 1).astype(bf16)
        (branch_mine if i < 2 else branch_other)[half, :] = branch


def attention_grad_kernel(
    branch_mine, branch_other, mine, other, gain, att, query, key, value, attended, log_total,
    cosine, sine, first, last, places,
    normed_mine, normed_other, grads, weight, normed, grad_qkv, grad_key, grad_value,
):
    shard = weight.shape[0] // 8
    for i in range(8):
        weight[i * shard : (i + 1) * shard, :] = att[i, :shard, :]
    for i in range(4):
        at = slice(i * ROWS, (i + 1) * ROWS)
        half = slice(i % 2 * ROWS, (i % 2 + 1) * ROWS)
        rows = (mine if i < 2 else other)[half, :]
        normed[at, :] = (rows.astype(f32) * gain[...]).astype(bf16)
        branch = (branch_mine if i < 2 else branch_other)[half, :]
        grad_att = contract(branch, weight[:, 3 * HEAD :], 1, 0).astype(bf16)
        scores = masked_scores(query[at, :], key[...], first[at, :], last[at, :], places[...])
        probs = jnp.exp(scores - log_total[at, :])
        grad_probs = contract(grad_att, value[...], 1, 1)
        inner = jnp.sum(probs * grad_probs, axis=1, keepdims=True)
        grad_scores = (probs * (grad_probs - inner)).astype(bf16)
        grad_query = contract(grad_scores, key[...], 1, 0) * HEAD ** (-0.5)
        grad_qkv[at, :HEAD] = rope_out(grad_query, cosine[at, :], sine[at, :]).astype(bf16)
        key_part = contract(grad_scores, query[at, :], 0, 0)
        value_part = contract(probs.astype(bf16), grad_att, 0, 0)
        if i == 0:
            grad_key[...] = key_part
            grad_value[...] = value_part
        else:
            grad_key[...] += key_part
            grad_value[...] += value_part
    grad_key_pre = rope_out(grad_key[...] * HEAD ** (-0.5), cosine[...], sine[...])
    grad_qkv[:, HEAD : 2 * HEAD] = grad_key_pre.astype(bf16)
    grad_qkv[:, 2 * HEAD :] = grad_value[...].astype(bf16)
    for i in range(4):
        at = slice(i * ROWS, (i + 1) * ROWS)
        half = slice(i % 2 * ROWS, (i % 2 + 1) * ROWS)
        rows = contract(grad_qkv[at, :], weight[:, : 3 * HEAD], 1, 1).astype(bf16)
        (normed_mine if i < 2 else normed_other)[half, :] = rows
    sums = jnp.sum(grad_qkv[...].astype(f32), axis=0, keepdims=True)
    sums = jnp.concatenate([sums, jnp.zeros((1, HEAD), f32)], axis=1)
    pad = jnp.where(lax.broadcasted_iota(jnp.int32, (16, 4 * HEAD), 0) == 0, sums, 0.0).astype(bf16)
    top = attended[: 2 * ROWS, :]
    low = attended[2 * ROWS :, :]
    for i in range(4):
        cols = slice(2 * i * shard, 2 * (i + 1) * shard)
        qkv_part = contract(normed[:, cols], grad_qkv[...], 0, 0)
        out_part = contract(branch_mine[:, cols], top, 0, 0)
        out_part += contract(branch_other[:, cols], low, 0, 0)
        both = jnp.concatenate([qkv_part, out_part], axis=1).astype(bf16)
        for j in range(2):
            base = (2 * i + j) * (shard + 16)
            grads[base : base + shard, :] = both[j * shard : (j + 1) * shard, :]
            grads[base + shard : base + shard + 16, :] = pad


def ffn_kernel(hi, rows, grad, weight_own, weight_far, hidden, grad_gu, grad_rows):
    width = weight_own.shape[0]
    units = weight_own.shape[1] // 3
    at_own = pl.ds(pl.multiple_of(hi[0] * width, HEAD), width)
    at_far = pl.ds(pl.multiple_of((1 - hi[0]) * width, HEAD), width)

    def product(left, cols):
        return contract(left[:, at_own], weight_own[:, cols], 1, 0) + contract(
            left[:, at_far], weight_far[:, cols], 1, 0
        )

    gate = product(rows, slice(0, units))
    upward = product(rows, slice(units, 2 * units))
    sigmoid = jax.nn.sigmoid(gate)
    activated = gate * sigmoid
    hidden[...] = (activated * upward).astype(bf16)
    grad_hidden = product(grad, slice(2 * units, 3 * units))
    grad_gu[:, :units] = (
        grad_hidden * upward * sigmoid * (1.0 + gate * (1.0 - sigmoid))
    ).astype(bf16)
    grad_gu[:, units:] = (grad_hidden * activated).astype(bf16)
    for at, weight in ((at_own, weight_own), (at_far, weight_far)):
        grad_rows[:, at] = contract(grad_gu[...], weight[:, : 2 * units], 1, 1).astype(bf16)


def output_kernel(hi, mine, other, weight_own, weight_far, out_mine, out_other):
    width = weight_own.shape[0]
    units = mine.shape[1]
    for weight, place in ((weight_own, hi[0]), (weight_far, 1 - hi[0])):
        at = pl.ds(pl.multiple_of(place * width, HEAD), width)
        for rows, out in ((other, out_other), (mine, out_mine)):
            out[:, at] = contract(rows[...], weight[:, 2 * units :], 1, 1).astype(bf16)


def down_grad_kernel(parts, out):
    start = 0
    for i in range(8):
        cols = (4 if i < 5 else 5) * BLOCK
        out[:, start : start + cols] = parts[i, :, :cols].astype(f32)
        start += cols


def gate_up_grad_kernel(parts, out):
    units = parts.shape[2] // 2
    start = 0
    for i in range(8):
        for j in range(4 if i < 5 else 5):
            for k in range(2):
                cols = slice(k * units + j * BLOCK, k * units + (j + 1) * BLOCK)
                out[:, k, start : start + BLOCK] = parts[i, :, cols].astype(f32)
            start += BLOCK


def attention_weight_grad_kernel(parts, grad_qkv, grad_out, sums, rest):
    shard = grad_qkv.shape[0]
    qcols = GROUP_Q * HEAD
    pairs = 0.0
    tails = 0.0
    for i in range(GROUP_Q):
        cols = slice(i * HEAD, (i + 1) * HEAD)
        grad_qkv[:, cols] = parts[i, :shard, :HEAD].astype(f32)
        grad_out[:, cols] = parts[i, :shard, 3 * HEAD :].astype(f32)
        tail = parts[i, shard:, :].astype(f32)
        sums[:, cols] = tail[:, :HEAD]
        pairs += parts[i, :shard, HEAD : 3 * HEAD].astype(f32)
        tails += tail[:, HEAD : 3 * HEAD]
    grad_qkv[:, qcols:] = pairs
    sums[:, qcols:] = tails
    rest[...] = sum(parts[i, shard:, :].astype(f32) for i in range(8))


def local_call(kernel, outs, scratch=()):
    return pl.pallas_call(
        kernel,
        out_shape=[jax.ShapeDtypeStruct(shape, dtype) for shape, dtype in outs],
        scratch_shapes=[pltpu.VMEM(shape, dtype) for shape, dtype in scratch],
        compiler_params=pltpu.CompilerParams(vmem_limit_bytes=VMEM_BYTES),
        cost_estimate=COST,
    )


def assemble(kernel, parts, outs):
    return local_call(kernel, outs)(parts)


def attention(mine, other, gain, att, bias, cosine, sine, first, last, places):
    half, width = mine.shape
    outs = [((2 * half, HEAD), bf16)] * 4 + [((2 * half, 1), f32)] + [((half, width), bf16)] * 2
    return local_call(attention_kernel, outs, [((width, 4 * HEAD), bf16)])(
        mine, other, gain, att, bias, cosine, sine, first, last, places
    )


def attention_grad(branch_mine, branch_other, mine, other, gain, att, *rest):
    half, width = mine.shape
    outs = [((half, width), bf16)] * 2 + [((width + 8 * 16, 4 * HEAD), bf16)]
    scratch = [
        ((width, 4 * HEAD), bf16),
        ((2 * half, width), bf16),
        ((2 * half, 3 * HEAD), bf16),
        ((2 * half, HEAD), f32),
        ((2 * half, HEAD), f32),
    ]
    return local_call(attention_grad_kernel, outs, scratch)(
        branch_mine, branch_other, mine, other, gain, att, *rest
    )


def output_rows(hi, rows, weight_own, weight_far):
    shape = (rows[0].shape[0], 2 * weight_own.shape[0])
    whole = [pl.BlockSpec(memory_space=pltpu.VMEM)] * 4
    return pl.pallas_call(
        output_kernel,
        in_specs=[pl.BlockSpec(memory_space=pltpu.SMEM)] + whole,
        out_specs=[pl.BlockSpec(memory_space=pltpu.VMEM)] * 2,
        out_shape=[jax.ShapeDtypeStruct(shape, bf16)] * 2,
        compiler_params=pltpu.CompilerParams(vmem_limit_bytes=VMEM_BYTES),
        cost_estimate=COST,
    )(hi, *rows, weight_own, weight_far)


def feed_forward(hi, rows, grad, weight_own, weight_far):
    count, width = rows.shape
    units = weight_own.shape[1] // 3

    def by_rows(cols):
        return pl.BlockSpec((ROWS, cols), lambda i, hi: (i, 0))

    whole = pl.BlockSpec(weight_own.shape, lambda i, hi: (0, 0))
    return pl.pallas_call(
        ffn_kernel,
        grid_spec=pltpu.PrefetchScalarGridSpec(
            num_scalar_prefetch=1,
            grid=(count // ROWS,),
            in_specs=[by_rows(width), by_rows(width), whole, whole],
            out_specs=[by_rows(units), by_rows(2 * units), by_rows(width)],
        ),
        out_shape=[
            jax.ShapeDtypeStruct((count, cols), bf16) for cols in (units, 2 * units, width)
        ],
        compiler_params=pltpu.CompilerParams(vmem_limit_bytes=VMEM_BYTES),
        cost_estimate=COST,
    )(hi, rows, grad, weight_own, weight_far)


def sequence_of(places, seq_lengths):
    ends = jnp.cumsum(seq_lengths)
    starts = ends - seq_lengths
    inside = (places[:, None] >= starts[None, :]) & (places[:, None] < ends[None, :])
    return jnp.sum(inside.astype(jnp.int32) * starts[None, :], axis=1)


def rotary(offset):
    half = HEAD // 2
    freqs = THETA ** (-(2.0 * jnp.arange(half, dtype=f32)) / HEAD)
    angle = offset.astype(f32)[:, None] * freqs[None, :]
    cosine, sine = jnp.cos(angle), jnp.sin(angle)
    return jnp.concatenate([cosine, cosine], axis=1), jnp.concatenate([-sine, sine], axis=1)


def rms_scale(values):
    return lax.rsqrt(jnp.mean(values * values, axis=-1, keepdims=True) + EPS)


def norm_back(values, scale, gain, incoming):
    weighted = incoming * gain
    return scale * weighted - values * scale**3 * jnp.mean(
        weighted * values, axis=-1, keepdims=True
    )


def on_device(
    tokens,
    cotangent,
    norm_attn,
    qkv_weight,
    qkv_bias,
    out_weight,
    norm_mlp,
    gate_up_weight,
    down_weight,
    lengths,
    deal,
):
    f = lax.axis_index("fsdp")
    c = lax.axis_index("ctx")
    t = lax.axis_index("tp")
    count, width = tokens.shape
    own = count // 2
    shard = qkv_weight.shape[0]
    qcols = GROUP_Q * HEAD
    has_head = c < GROUP_Q
    head = jnp.minimum(c, GROUP_Q - 1)

    tok = lax.dynamic_slice_in_dim(tokens, t * own, own)
    cot = lax.dynamic_slice_in_dim(cotangent, t * own, own)
    scale_a = rms_scale(tok)
    unit_own = (tok * scale_a).astype(bf16)
    grad_own = cot.astype(bf16)

    w_out_own = lax.dynamic_slice_in_dim(out_weight, head * HEAD, HEAD).T
    w_out_own = jnp.where(has_head, w_out_own, jnp.zeros_like(w_out_own))
    att_own = jnp.concatenate(
        [
            lax.dynamic_slice_in_dim(qkv_weight, head * HEAD, HEAD, axis=1),
            qkv_weight[:, qcols:],
            w_out_own,
        ],
        axis=1,
    )
    row = jnp.concatenate([norm_attn, norm_mlp, qkv_bias[0]])[None]
    att_own = jnp.concatenate([att_own, row, jnp.zeros((15, row.shape[1]), bf16)], axis=0)
    att_far = lax.ppermute(att_own, "fsdp", XH_SWAP)

    start = jnp.maximum(4 * c, 5 * c - 5) * BLOCK
    units = 5 * BLOCK
    gu_own = lax.dynamic_slice_in_dim(gate_up_weight, start, units, axis=2)
    inside = (jnp.arange(units) < 4 * BLOCK) | (c >= 5)
    gu_own = jnp.where(inside, gu_own, jnp.zeros_like(gu_own))
    down_own = lax.dynamic_slice_in_dim(down_weight, start, units).T
    ffn_own = jnp.concatenate([gu_own[:, 0], gu_own[:, 1], down_own], axis=1)
    ffn_line = gather_along_y(ffn_own)

    att_all = gather_small(att_own, att_far)
    extra = att_all[:, shard].astype(f32)
    gain_a = extra[:, :shard].reshape(1, width)
    gain_m = extra[:, shard : 2 * shard].reshape(1, width)
    bias_all = extra[:, 2 * shard :].reshape(1, -1)
    bias = jnp.concatenate(
        [lax.dynamic_slice_in_dim(bias_all, head * HEAD, HEAD, axis=1), bias_all[:, qcols:]], axis=1
    )

    deal_all = deal[0].reshape(8, 2, own)[:, t ^ jnp.arange(2)]
    places = jnp.transpose(deal_all, (1, 0, 2)).reshape(-1)
    first = sequence_of(places, lengths[0])
    cosine, sine = rotary(places - first)
    order = (cosine, sine, first[:, None], places[:, None], places[None, :])

    ffn_far = lax.ppermute(ffn_own, "fsdp", XH_SWAP)
    unit_mine, att_all, grad_own, ffn_line, ffn_far, *order = tie(
        gather(unit_own, "ctx"), att_all, grad_own, ffn_line, ffn_far, *order
    )
    ffn_far = gather_along_y(ffn_far)
    grad_mine = gather(grad_own, "ctx")
    units_all = both_cores(unit_mine)
    held = attention(*units_all, gain_a, att_all, bias, *order)
    *held, grad_mine = tie(*held, grad_mine)
    query, key, value, attended, log_total, branch_mine, branch_other = held
    grads = both_cores(grad_mine)
    branch_parts = pair_sums(branch_mine, branch_other)
    branch = summed(spread(branch_parts, "ctx"))
    middle = tok + branch
    scale_m = rms_scale(middle)
    normed2_mine = gather((middle * scale_m * gain_m).astype(bf16), "ctx")
    normed2_mine, ffn_far, *grads = tie(normed2_mine, ffn_far, *grads)
    normed2 = both_cores(normed2_mine)

    hi = (f // 4)[None]
    hidden, grad_gu, parts = zip(
        *[feed_forward(hi, r, g, ffn_line, ffn_far) for r, g in zip(normed2, grads)]
    )
    parts = pair_sums(*parts)
    parts, *held = tie(parts, *normed2, *grad_gu, *hidden, *grads)
    normed2, grad_gu, hidden, grads = held[0:2], held[2:4], held[4:6], held[6:8]
    normed2_parts = spread(parts, "ctx")

    gu_blocks, *held = tie(by_y(over_rows(normed2, grad_gu)), *grads, *hidden)
    grads, hidden = held[:2], held[2:]
    gu_sums = reduce_along_y(gu_blocks)
    output_parts = pair_sums(*output_rows(hi, hidden, ffn_line, ffn_far))
    normed2_parts, down_blocks, output_parts = tie(
        normed2_parts, by_y(over_rows(grads, hidden)), output_parts
    )
    down_sums = reduce_along_y(down_blocks)

    grad_middle = cot + norm_back(middle, scale_m, gain_m, summed(normed2_parts))
    gu_kept, gu_got = swap_over_hi(gu_sums)
    branch_mine, gu_kept, gu_got, output_parts = tie(
        gather(grad_middle.astype(bf16), "ctx"), gu_kept, gu_got, output_parts
    )
    output_pair = lax.psum_scatter(
        output_parts.reshape(-1, width),
        "ctx",
        scatter_dimension=0,
        axis_index_groups=Z_GROUPS,
        tiled=True,
    ).reshape(2, own, width)
    gu_share = added(gu_kept, gu_got)
    gu_far = lax.ppermute(gu_share, "ctx", XL_SWAP)
    grad_branch = both_cores(branch_mine)
    normed_mine, normed_other, att_grads = attention_grad(
        *grad_branch, *units_all, gain_a, att_all, query, key, value, attended, log_total, *order
    )
    att_grads, gu_far, down_sums = tie(att_grads, gu_far, down_sums)
    att_parts = spread(att_grads.reshape(8, -1, 4 * HEAD), "fsdp")
    gu_part = gather_along_z(ordered(gu_share, gu_far, c % 2)).reshape(8, shard, -1)
    normed_parts = pair_sums(normed_mine, normed_other)
    down_kept, down_got = swap_over_hi(down_sums)
    gain_part = jnp.sum(gu_share.astype(f32) * ffn_own[:, : 2 * units].astype(f32), axis=1)
    gain_row = jnp.pad(gain_part.astype(bf16)[None], ((shard + 1, 14), (0, 4 * HEAD - shard)))
    att_parts, down_kept, down_got, gain_row, normed_parts, output_pair = tie(
        att_parts, down_kept, down_got, gain_row, normed_parts, output_pair
    )
    att_part = gather((summed(att_parts) + gain_row).astype(bf16), "ctx")
    output_kept = jnp.where(c % 2 == 0, output_pair[0], output_pair[1])
    output_sent = jnp.where(c % 2 == 0, output_pair[1], output_pair[0])
    output_got = lax.ppermute(output_sent, "ctx", XL_SWAP)
    down_share = added(down_kept, down_got)
    down_far = lax.ppermute(down_share, "ctx", XL_SWAP)
    att_part, down_share, down_far, output_kept, output_got, normed_parts = tie(
        att_part, down_share, down_far, output_kept, output_got, normed_parts
    )
    output = both_halves(middle + output_kept.astype(f32) + output_got.astype(f32))
    down_part = gather_along_z(ordered(down_share, down_far, c % 2)).reshape(8, shard, units)
    normed_parts = spread(normed_parts, "ctx")
    grad_tokens = both_halves(
        grad_middle + norm_back(tok, scale_a, gain_a, summed(normed_parts))
    )
    grad_down_weight = assemble(
        down_grad_kernel, down_part, [((shard, down_weight.shape[0]), f32)]
    )[0]
    grad_gu_weight = pl.pallas_call(
        gate_up_grad_kernel,
        grid=(shard // GRAD_ROWS,),
        in_specs=[pl.BlockSpec((8, GRAD_ROWS, 2 * units), lambda i: (0, i, 0))],
        out_specs=pl.BlockSpec((GRAD_ROWS,) + gate_up_weight.shape[1:], lambda i: (i, 0, 0)),
        out_shape=jax.ShapeDtypeStruct(gate_up_weight.shape, f32),
        compiler_params=pltpu.CompilerParams(vmem_limit_bytes=VMEM_BYTES),
        cost_estimate=COST,
    )(gu_part)
    grad_qkv_weight, grad_out_weight, sums, rest = assemble(
        attention_weight_grad_kernel,
        att_part,
        [
            (qkv_weight.shape, f32),
            ((shard, qcols), f32),
            ((16, qkv_weight.shape[1]), f32),
            ((16, 4 * HEAD), f32),
        ],
    )
    split_at = qcols + HEAD
    own_bias = lax.dynamic_slice(sums, (0, f * (split_at // 8)), (1, split_at // 8))
    own_value = lax.dynamic_slice(sums, (0, split_at + f * (HEAD // 8)), (1, HEAD // 8))
    gain_sums = jnp.stack(
        [
            jnp.sum(grad_qkv_weight * qkv_weight.astype(f32), axis=1) / norm_attn.astype(f32),
            rest[1, :shard] / norm_mlp.astype(f32),
        ]
    )
    gain_sums = gain_sums + lax.ppermute(gain_sums, "tp", TP_SWAP)

    return (
        output,
        grad_tokens,
        gain_sums[0],
        grad_qkv_weight,
        own_bias,
        own_value,
        grad_out_weight.T,
        gain_sums[1],
        grad_gu_weight,
        grad_down_weight.T,
    )


def solution(mesh):
    in_specs = (
        P(("fsdp", "ctx"), None),
        P(("fsdp", "ctx"), None),
        P("fsdp"),
        P("fsdp", "tp"),
        P("tp", "fsdp"),
        P("tp", "fsdp"),
        P("fsdp"),
        P("fsdp", None, "tp"),
        P("tp", "fsdp"),
        P("fsdp", None),
        P("fsdp", None),
    )
    out_specs = (
        P(("fsdp", "ctx"), None),
        P(("fsdp", "ctx"), None),
        P("fsdp"),
        P("fsdp", "tp"),
        P("tp", "fsdp"),
        P("tp", "fsdp"),
        P("tp", "fsdp"),
        P("fsdp"),
        P("fsdp", None, "tp"),
        P("tp", "fsdp"),
    )
    return jax.shard_map(
        on_device, mesh=mesh, in_specs=in_specs, out_specs=out_specs, check_vma=False
    )
```

```python
import jax
import jax.numpy as jnp
from jax import lax
from jax.experimental import pallas as pl
from jax.experimental.pallas import tpu as pltpu
from jax.sharding import PartitionSpec as P

HEAD = 128
GROUP_Q = 6
EPS = 1e-06
THETA = 1000000.0

bf16 = jnp.bfloat16
f32 = jnp.float32

BLOCK = 128
ROWS = 256
GRAD_ROWS = 64
VMEM_BYTES = 60 * 2**20
COST = pl.CostEstimate(flops=10**6, bytes_accessed=10**5, transcendentals=0)

TP_SWAP = [(0, 1), (1, 0)]
XH_SWAP = [(i, i ^ 4) for i in range(8)]
XL_SWAP = [(i, i ^ 1) for i in range(8)]
Y_GROUPS = [[0, 1, 2, 3], [4, 5, 6, 7]]
Z_GROUPS = [[0, 2, 4, 6], [1, 3, 5, 7]]


def y_shift(k):
    return [(h * 4 + y, h * 4 + (y + k) % 4) for h in range(2) for y in range(4)]


def contract(left, right, left_dim, right_dim):
    return lax.dot_general(
        left, right, (((left_dim,), (right_dim,)), ((), ())), preferred_element_type=f32
    )


def tie(*values):
    return lax.optimization_barrier(values)


def ordered(own, other, place):
    return jnp.stack([jnp.where(place == 0, own, other), jnp.where(place == 0, other, own)])


def gather(own, axis):
    copies = jnp.broadcast_to(own[None], (8,) + own.shape)
    return lax.all_to_all(copies, axis, 0, 0, tiled=True)


def spread(part, axis):
    return lax.all_to_all(part, axis, 0, 0, tiled=True)


def spread_along_z(part):
    return lax.all_to_all(part, "ctx", 0, 0, tiled=True, axis_index_groups=Z_GROUPS)


def summed(parts):
    return jnp.sum(parts.astype(f32), axis=0)


def gather_small(own, far):
    me = lax.axis_index("fsdp")
    hi, y = me // 4, me % 4
    out = jnp.zeros((8,) + own.shape, own.dtype)
    for d, base in ((0, own), (1, far)):
        out = lax.dynamic_update_index_in_dim(out, base, (hi ^ d) * 4 + y, 0)
        for k in (1, 3, 2):
            piece = lax.ppermute(base, "fsdp", y_shift(k))
            out = lax.dynamic_update_index_in_dim(out, piece, (hi ^ d) * 4 + (y - k + 4) % 4, 0)
    return out


def gather_along_y(own):
    return lax.all_gather(own, "fsdp", axis=0, axis_index_groups=Y_GROUPS, tiled=True)


def by_y(part):
    rows, width = part.shape
    return jnp.swapaxes(part.astype(bf16).reshape(2, 4, -1, width), 0, 1).reshape(rows, width)


def reduce_along_y(part):
    pair = lax.psum_scatter(
        part, "fsdp", scatter_dimension=0, axis_index_groups=Y_GROUPS, tiled=True
    )
    return pair.reshape(2, -1, part.shape[1])


def swap_over_hi(pair):
    hi = lax.axis_index("fsdp") // 4
    sent = jnp.where(hi == 0, pair[1], pair[0])
    return jnp.where(hi == 0, pair[0], pair[1]), lax.ppermute(sent, "fsdp", XH_SWAP)


def added(kept, got):
    return (kept.astype(f32) + got.astype(f32)).astype(bf16)


def gather_along_z(own):
    return lax.all_gather(own, "ctx", axis=0, axis_index_groups=Z_GROUPS)


def both_cores(mine):
    mine = mine.reshape(-1, mine.shape[-1])
    return [mine, lax.ppermute(mine, "tp", TP_SWAP)]


def pair_sums(mine, other):
    got = lax.ppermute(other, "tp", TP_SWAP)
    total = (mine.astype(f32) + got.astype(f32)).astype(bf16)
    return total.reshape(8, -1, total.shape[1])


def over_rows(lefts, rights):
    return contract(lefts[0], rights[0], 0, 0) + contract(lefts[1], rights[1], 0, 0)


def both_halves(own):
    t = lax.axis_index("tp")
    other = lax.ppermute(own, "tp", TP_SWAP)
    first = jnp.where(t == 0, own, other)
    second = jnp.where(t == 0, other, own)
    return jnp.concatenate([first, second], axis=0)


def rope_in(values, cosine, sine):
    return values * cosine + pltpu.roll(values, HEAD // 2, 1) * sine


def rope_out(grads, cosine, sine):
    return grads * cosine - pltpu.roll(grads, HEAD // 2, 1) * sine


def masked_scores(query, key, ends, places):
    scores = contract(query, key, 1, 1) * HEAD ** (-0.5)
    first, last = ends[:, :1], ends[:, HEAD // 2 : HEAD // 2 + 1]
    return jnp.where((places >= first) & (places <= last), scores, -1e30)


def attention_kernel(
    mine, other, gain, att, bias, cosine, sine, ends, places,
    query, key, value, attended, log_total, branch_mine, branch_other, weight,
):
    shard = weight.shape[0] // 8
    for i in range(8):
        weight[i * shard : (i + 1) * shard, :] = att[i, :shard, :]
    for i in range(4):
        at = slice(i * ROWS, (i + 1) * ROWS)
        half = slice(i % 2 * ROWS, (i % 2 + 1) * ROWS)
        rows = (mine if i < 2 else other)[half, :]
        normed = (rows.astype(f32) * gain[...]).astype(bf16)
        qkv = contract(normed, weight[:, : 3 * HEAD], 1, 0) + bias[...]
        query[at, :] = rope_in(qkv[:, :HEAD], cosine[at, :], sine[at, :]).astype(bf16)
        key[at, :] = rope_in(qkv[:, HEAD : 2 * HEAD], cosine[at, :], sine[at, :]).astype(bf16)
        value[at, :] = qkv[:, 2 * HEAD :].astype(bf16)
    for i in range(4):
        at = slice(i * ROWS, (i + 1) * ROWS)
        half = slice(i % 2 * ROWS, (i % 2 + 1) * ROWS)
        scores = masked_scores(query[at, :], key[...], ends[at, :], places[...])
        top = jnp.max(scores, axis=1, keepdims=True)
        raised = jnp.exp(scores - top)
        total = jnp.sum(raised, axis=1, keepdims=True)
        log_total[at, :] = top + jnp.log(total)
        probs = (raised / total).astype(bf16)
        rows = contract(probs, value[...], 1, 0).astype(bf16)
        attended[at, :] = rows
        branch = contract(rows, weight[:, 3 * HEAD :], 1, 1).astype(bf16)
        (branch_mine if i < 2 else branch_other)[half, :] = branch


def attention_grad_kernel(
    branch_mine, branch_other, mine, other, gain, att, query, key, value, attended, log_total,
    cosine, sine, ends, places,
    normed_mine, normed_other, grads, weight, normed, grad_qkv, grad_key, grad_value,
):
    shard = weight.shape[0] // 8
    for i in range(8):
        weight[i * shard : (i + 1) * shard, :] = att[i, :shard, :]
    for i in range(4):
        at = slice(i * ROWS, (i + 1) * ROWS)
        half = slice(i % 2 * ROWS, (i % 2 + 1) * ROWS)
        rows = (mine if i < 2 else other)[half, :]
        normed[at, :] = (rows.astype(f32) * gain[...]).astype(bf16)
        branch = (branch_mine if i < 2 else branch_other)[half, :]
        grad_att = contract(branch, weight[:, 3 * HEAD :], 1, 0).astype(bf16)
        scores = masked_scores(query[at, :], key[...], ends[at, :], places[...])
        probs = jnp.exp(scores - log_total[at, :])
        grad_probs = contract(grad_att, value[...], 1, 1)
        inner = jnp.sum(probs * grad_probs, axis=1, keepdims=True)
        grad_scores = (probs * (grad_probs - inner)).astype(bf16)
        grad_query = contract(grad_scores, key[...], 1, 0) * HEAD ** (-0.5)
        grad_qkv[at, :HEAD] = rope_out(grad_query, cosine[at, :], sine[at, :]).astype(bf16)
        key_part = contract(grad_scores, query[at, :], 0, 0)
        value_part = contract(probs.astype(bf16), grad_att, 0, 0)
        if i == 0:
            grad_key[...] = key_part
            grad_value[...] = value_part
        else:
            grad_key[...] += key_part
            grad_value[...] += value_part
    grad_key_pre = rope_out(grad_key[...] * HEAD ** (-0.5), cosine[...], sine[...])
    grad_qkv[:, HEAD : 2 * HEAD] = grad_key_pre.astype(bf16)
    grad_qkv[:, 2 * HEAD :] = grad_value[...].astype(bf16)
    for i in range(4):
        at = slice(i * ROWS, (i + 1) * ROWS)
        half = slice(i % 2 * ROWS, (i % 2 + 1) * ROWS)
        rows = contract(grad_qkv[at, :], weight[:, : 3 * HEAD], 1, 1).astype(bf16)
        (normed_mine if i < 2 else normed_other)[half, :] = rows
    sums = jnp.sum(grad_qkv[...].astype(f32), axis=0, keepdims=True)
    sums = jnp.concatenate([sums, jnp.zeros((1, HEAD), f32)], axis=1)
    pad = jnp.where(lax.broadcasted_iota(jnp.int32, (16, 4 * HEAD), 0) == 0, sums, 0.0).astype(bf16)
    top = attended[: 2 * ROWS, :]
    low = attended[2 * ROWS :, :]
    for i in range(4):
        cols = slice(2 * i * shard, 2 * (i + 1) * shard)
        qkv_part = contract(normed[:, cols], grad_qkv[...], 0, 0)
        out_part = contract(branch_mine[:, cols], top, 0, 0)
        out_part += contract(branch_other[:, cols], low, 0, 0)
        both = jnp.concatenate([qkv_part, out_part], axis=1).astype(bf16)
        for j in range(2):
            base = (2 * i + j) * (shard + 16)
            grads[base : base + shard, :] = both[j * shard : (j + 1) * shard, :]
            grads[base + shard : base + shard + 16, :] = pad


def ffn_kernel(hi, rows, grad, weight_own, weight_far, hidden, grad_gu, grad_rows):
    width = weight_own.shape[0]
    units = weight_own.shape[1] // 3
    at_own = pl.ds(pl.multiple_of(hi[0] * width, HEAD), width)
    at_far = pl.ds(pl.multiple_of((1 - hi[0]) * width, HEAD), width)

    def product(left, cols):
        return contract(left[:, at_own], weight_own[:, cols], 1, 0) + contract(
            left[:, at_far], weight_far[:, cols], 1, 0
        )

    gate = product(rows, slice(0, units))
    upward = product(rows, slice(units, 2 * units))
    sigmoid = jax.nn.sigmoid(gate)
    activated = gate * sigmoid
    hidden[...] = (activated * upward).astype(bf16)
    grad_hidden = product(grad, slice(2 * units, 3 * units))
    grad_gu[:, :units] = (
        grad_hidden * upward * sigmoid * (1.0 + gate * (1.0 - sigmoid))
    ).astype(bf16)
    grad_gu[:, units:] = (grad_hidden * activated).astype(bf16)
    for at, weight in ((at_own, weight_own), (at_far, weight_far)):
        grad_rows[:, at] = contract(grad_gu[...], weight[:, : 2 * units], 1, 1).astype(bf16)


def weight_grad_kernel(left_mine, left_other, right_mine, right_other, out):
    shard = left_mine.shape[1] // 8
    for i in range(4):
        cols = slice(2 * i * shard, 2 * (i + 1) * shard)
        part = contract(left_mine[:, cols], right_mine[...], 0, 0)
        part += contract(left_other[:, cols], right_other[...], 0, 0)
        for j in range(2):
            base = ((2 * i + j) % 4 * 2 + (2 * i + j) // 4) * shard
            out[base : base + shard, :] = part[j * shard : (j + 1) * shard, :].astype(bf16)


def output_kernel(hi, mine, other, weight_own, weight_far, out_mine, out_other):
    width = weight_own.shape[0]
    units = mine.shape[1]
    for weight, place in ((weight_own, hi[0]), (weight_far, 1 - hi[0])):
        at = pl.ds(pl.multiple_of(place * width, HEAD), width)
        for rows, out in ((other, out_other), (mine, out_mine)):
            out[:, at] = contract(rows[...], weight[:, 2 * units :], 1, 1).astype(bf16)


def down_grad_kernel(parts, out):
    start = 0
    for i in range(8):
        cols = (4 if i < 5 else 5) * BLOCK
        out[:, start : start + cols] = parts[i, :, :cols].astype(f32)
        start += cols


def gate_up_grad_kernel(parts, out):
    units = parts.shape[2] // 2
    start = 0
    for i in range(8):
        for j in range(4 if i < 5 else 5):
            for k in range(2):
                cols = slice(k * units + j * BLOCK, k * units + (j + 1) * BLOCK)
                out[:, k, start : start + BLOCK] = parts[i, :, cols].astype(f32)
            start += BLOCK


def attention_weight_grad_kernel(parts, grad_qkv, grad_out, sums, rest):
    shard = grad_qkv.shape[0]
    qcols = GROUP_Q * HEAD
    pairs = 0.0
    tails = 0.0
    for i in range(GROUP_Q):
        cols = slice(i * HEAD, (i + 1) * HEAD)
        grad_qkv[:, cols] = parts[i, :shard, :HEAD].astype(f32)
        grad_out[:, cols] = parts[i, :shard, 3 * HEAD :].astype(f32)
        tail = parts[i, shard:, :].astype(f32)
        sums[:, cols] = tail[:, :HEAD]
        pairs += parts[i, :shard, HEAD : 3 * HEAD].astype(f32)
        tails += tail[:, HEAD : 3 * HEAD]
    grad_qkv[:, qcols:] = pairs
    sums[:, qcols:] = tails
    rest[...] = sum(parts[i, shard:, :].astype(f32) for i in range(8))


def local_call(kernel, outs, scratch=()):
    return pl.pallas_call(
        kernel,
        out_shape=[jax.ShapeDtypeStruct(shape, dtype) for shape, dtype in outs],
        scratch_shapes=[pltpu.VMEM(shape, dtype) for shape, dtype in scratch],
        compiler_params=pltpu.CompilerParams(vmem_limit_bytes=VMEM_BYTES),
        cost_estimate=COST,
    )


def assemble(kernel, parts, outs):
    return local_call(kernel, outs)(parts)


def attention(mine, other, gain, att, bias, cosine, sine, ends, places):
    half, width = mine.shape
    outs = [((2 * half, HEAD), bf16)] * 4 + [((2 * half, 1), f32)] + [((half, width), bf16)] * 2
    return local_call(attention_kernel, outs, [((width, 4 * HEAD), bf16)])(
        mine, other, gain, att, bias, cosine, sine, ends, places
    )


def attention_grad(branch_mine, branch_other, mine, other, gain, att, *rest):
    half, width = mine.shape
    outs = [((half, width), bf16)] * 2 + [((width + 8 * 16, 4 * HEAD), bf16)]
    scratch = [
        ((width, 4 * HEAD), bf16),
        ((2 * half, width), bf16),
        ((2 * half, 3 * HEAD), bf16),
        ((2 * half, HEAD), f32),
        ((2 * half, HEAD), f32),
    ]
    return local_call(attention_grad_kernel, outs, scratch)(
        branch_mine, branch_other, mine, other, gain, att, *rest
    )


def weight_grad(lefts, rights):
    outs = [((lefts[0].shape[1], rights[0].shape[1]), bf16)]
    return local_call(weight_grad_kernel, outs)(*lefts, *rights)[0]


def output_rows(hi, rows, weight_own, weight_far):
    shape = (rows[0].shape[0], 2 * weight_own.shape[0])
    whole = [pl.BlockSpec(memory_space=pltpu.VMEM)] * 4
    return pl.pallas_call(
        output_kernel,
        in_specs=[pl.BlockSpec(memory_space=pltpu.SMEM)] + whole,
        out_specs=[pl.BlockSpec(memory_space=pltpu.VMEM)] * 2,
        out_shape=[jax.ShapeDtypeStruct(shape, bf16)] * 2,
        compiler_params=pltpu.CompilerParams(vmem_limit_bytes=VMEM_BYTES),
        cost_estimate=COST,
    )(hi, *rows, weight_own, weight_far)


def feed_forward(hi, rows, grad, weight_own, weight_far):
    count, width = rows.shape
    units = weight_own.shape[1] // 3

    def by_rows(cols):
        return pl.BlockSpec((ROWS, cols), lambda i, hi: (i, 0))

    whole = pl.BlockSpec(weight_own.shape, lambda i, hi: (0, 0))
    return pl.pallas_call(
        ffn_kernel,
        grid_spec=pltpu.PrefetchScalarGridSpec(
            num_scalar_prefetch=1,
            grid=(count // ROWS,),
            in_specs=[by_rows(width), by_rows(width), whole, whole],
            out_specs=[by_rows(units), by_rows(2 * units), by_rows(width)],
        ),
        out_shape=[
            jax.ShapeDtypeStruct((count, cols), bf16) for cols in (units, 2 * units, width)
        ],
        compiler_params=pltpu.CompilerParams(vmem_limit_bytes=VMEM_BYTES),
        cost_estimate=COST,
    )(hi, rows, grad, weight_own, weight_far)


def sequence_of(places, seq_lengths):
    ends = jnp.cumsum(seq_lengths)
    starts = ends - seq_lengths
    inside = (places[:, None] >= starts[None, :]) & (places[:, None] < ends[None, :])
    return jnp.sum(inside.astype(jnp.int32) * starts[None, :], axis=1)


def rotary(offset):
    half = HEAD // 2
    freqs = THETA ** (-(2.0 * jnp.arange(half, dtype=f32)) / HEAD)
    angle = offset.astype(f32)[:, None] * freqs[None, :]
    cosine, sine = jnp.cos(angle), jnp.sin(angle)
    return jnp.concatenate([cosine, cosine], axis=1), jnp.concatenate([-sine, sine], axis=1)


def rms_scale(values):
    return lax.rsqrt(jnp.mean(values * values, axis=-1, keepdims=True) + EPS)


def norm_back(values, scale, gain, incoming):
    weighted = incoming * gain
    return scale * weighted - values * scale**3 * jnp.mean(
        weighted * values, axis=-1, keepdims=True
    )


def on_device(
    tokens,
    cotangent,
    norm_attn,
    qkv_weight,
    qkv_bias,
    out_weight,
    norm_mlp,
    gate_up_weight,
    down_weight,
    lengths,
    deal,
):
    f = lax.axis_index("fsdp")
    c = lax.axis_index("ctx")
    t = lax.axis_index("tp")
    count, width = tokens.shape
    own = count // 2
    shard = qkv_weight.shape[0]
    qcols = GROUP_Q * HEAD
    has_head = c < GROUP_Q
    head = jnp.minimum(c, GROUP_Q - 1)

    tok = lax.dynamic_slice_in_dim(tokens, t * own, own)
    cot = lax.dynamic_slice_in_dim(cotangent, t * own, own)
    scale_a = rms_scale(tok)
    unit_own = (tok * scale_a).astype(bf16)
    grad_own = cot.astype(bf16)

    w_out_own = lax.dynamic_slice_in_dim(out_weight, head * HEAD, HEAD).T
    w_out_own = jnp.where(has_head, w_out_own, jnp.zeros_like(w_out_own))
    att_own = jnp.concatenate(
        [
            lax.dynamic_slice_in_dim(qkv_weight, head * HEAD, HEAD, axis=1),
            qkv_weight[:, qcols:],
            w_out_own,
        ],
        axis=1,
    )
    row = jnp.concatenate([norm_attn, norm_mlp, qkv_bias[0]])[None]
    att_own = jnp.concatenate([att_own, row, jnp.zeros((15, row.shape[1]), bf16)], axis=0)
    att_far = lax.ppermute(att_own, "fsdp", XH_SWAP)

    start = jnp.maximum(4 * c, 5 * c - 5) * BLOCK
    units = 5 * BLOCK
    gu_own = lax.dynamic_slice_in_dim(gate_up_weight, start, units, axis=2)
    inside = (jnp.arange(units) < 4 * BLOCK) | (c >= 5)
    gu_own = jnp.where(inside, gu_own, jnp.zeros_like(gu_own))
    down_own = lax.dynamic_slice_in_dim(down_weight, start, units).T
    ffn_own = jnp.concatenate([gu_own[:, 0], gu_own[:, 1], down_own], axis=1)

    att_all = gather_small(att_own, att_far)
    extra = att_all[:, shard].astype(f32)
    gain_a = extra[:, :shard].reshape(1, width)
    gain_m = extra[:, shard : 2 * shard].reshape(1, width)
    bias_all = extra[:, 2 * shard :].reshape(1, -1)
    bias = jnp.concatenate(
        [lax.dynamic_slice_in_dim(bias_all, head * HEAD, HEAD, axis=1), bias_all[:, qcols:]], axis=1
    )

    deal_all = deal[0].reshape(8, 2, own)[:, t ^ jnp.arange(2)]
    places = jnp.transpose(deal_all, (1, 0, 2)).reshape(-1)
    first = sequence_of(places, lengths[0])
    cosine, sine = rotary(places - first)
    ends = jnp.where(jnp.arange(HEAD) < HEAD // 2, first[:, None], places[:, None])
    order = (cosine, sine, ends, places[None, :])

    grad_far = lax.ppermute(grad_own, "ctx", XL_SWAP)
    unit_mine, att_all, grad_own, grad_far, ffn_own, *order = tie(
        gather(unit_own, "ctx"), att_all, grad_own, grad_far, ffn_own, *order
    )
    ffn_far = lax.ppermute(ffn_own, "fsdp", XH_SWAP)
    ffn_line = gather_along_y(ffn_own)
    grad_pair = ordered(grad_own, grad_far, c % 2)
    grad_mine = spread_along_z(jnp.broadcast_to(grad_pair[None], (4,) + grad_pair.shape))
    units_all = both_cores(unit_mine)
    held = attention(*units_all, gain_a, att_all, bias, *order)
    *held, grad_mine, ffn_far = tie(*held, grad_mine, ffn_far)
    query, key, value, attended, log_total, branch_mine, branch_other = held
    ffn_far = gather_along_y(ffn_far)
    branch_parts = pair_sums(branch_mine, branch_other)
    grads = both_cores(grad_mine)
    branch = summed(spread(branch_parts, "ctx"))
    middle = tok + branch
    scale_m = rms_scale(middle)
    normed2_mine = gather((middle * scale_m * gain_m).astype(bf16), "ctx")
    normed2_mine, ffn_line, ffn_far, *grads = tie(normed2_mine, ffn_line, ffn_far, *grads)
    normed2 = both_cores(normed2_mine)

    hi = (f // 4)[None]
    hidden, grad_gu, parts = zip(
        *[feed_forward(hi, r, g, ffn_line, ffn_far) for r, g in zip(normed2, grads)]
    )
    parts = pair_sums(*parts)
    parts, *held = tie(parts, *normed2, *grad_gu, *hidden, *grads)
    normed2, grad_gu, hidden, grads = held[0:2], held[2:4], held[4:6], held[6:8]
    normed2_parts = spread(parts, "ctx")

    gu_blocks, *held = tie(by_y(over_rows(normed2, grad_gu)), *grads, *hidden)
    grads, hidden = held[:2], held[2:]
    gu_sums = reduce_along_y(gu_blocks)
    normed2_parts, down_blocks, *output_raw = tie(
        normed2_parts,
        weight_grad(grads, hidden),
        *output_rows(hi, hidden, ffn_line, ffn_far),
    )
    down_sums = reduce_along_y(down_blocks)

    grad_middle = cot + norm_back(middle, scale_m, gain_m, summed(normed2_parts))
    output_parts = pair_sums(*output_raw)
    gu_kept, gu_got = swap_over_hi(gu_sums)
    branch_mine, gu_kept, gu_got, output_parts = tie(
        gather(grad_middle.astype(bf16), "ctx"), gu_kept, gu_got, output_parts
    )
    output_parts = spread_along_z(output_parts.reshape(4, 2 * own, width))
    gu_share = added(gu_kept, gu_got)
    gu_far = lax.ppermute(gu_share, "ctx", XL_SWAP)
    grad_branch = both_cores(branch_mine)
    normed_mine, normed_other, att_grads = attention_grad(
        *grad_branch, *units_all, gain_a, att_all, query, key, value, attended, log_total, *order
    )
    att_grads, gu_far, output_parts = tie(att_grads, gu_far, output_parts)
    output_pair = summed(output_parts).reshape(2, own, width)
    output_kept = jnp.where(c % 2 == 0, output_pair[0], output_pair[1])
    output_sent = jnp.where(c % 2 == 0, output_pair[1], output_pair[0]).astype(bf16)
    output_got = lax.ppermute(output_sent, "ctx", XL_SWAP)
    att_parts = spread(att_grads.reshape(8, -1, 4 * HEAD), "fsdp")
    gu_part = gather_along_z(ordered(gu_share, gu_far, c % 2)).reshape(8, shard, -1)
    normed_parts = pair_sums(normed_mine, normed_other)
    gain_part = jnp.sum(gu_share.astype(f32) * ffn_own[:, : 2 * units].astype(f32), axis=1)
    gain_row = jnp.pad(gain_part.astype(bf16)[None], ((shard + 1, 14), (0, 4 * HEAD - shard)))
    att_parts, down_sums, gain_row, normed_parts, output_kept, output_got = tie(
        att_parts, down_sums, gain_row, normed_parts, output_kept, output_got
    )
    att_part = gather((summed(att_parts) + gain_row).astype(bf16), "ctx")
    down_kept, down_got = swap_over_hi(down_sums)
    att_part, down_kept, down_got, normed_parts = tie(
        att_part, down_kept, down_got, normed_parts
    )
    down_share = added(down_kept, down_got)
    down_pair = ordered(down_share, lax.ppermute(down_share, "ctx", XL_SWAP), c % 2)
    down_part = gather_along_z(down_pair).reshape(8, shard, units)
    output = both_halves(middle + output_kept + output_got.astype(f32))
    grad_gu_weight = pl.pallas_call(
        gate_up_grad_kernel,
        grid=(shard // GRAD_ROWS,),
        in_specs=[pl.BlockSpec((8, GRAD_ROWS, 2 * units), lambda i: (0, i, 0))],
        out_specs=pl.BlockSpec((GRAD_ROWS,) + gate_up_weight.shape[1:], lambda i: (i, 0, 0)),
        out_shape=jax.ShapeDtypeStruct(gate_up_weight.shape, f32),
        compiler_params=pltpu.CompilerParams(vmem_limit_bytes=VMEM_BYTES),
        cost_estimate=COST,
    )(gu_part)
    normed_parts, grad_gu_weight = tie(spread(normed_parts, "ctx"), grad_gu_weight)
    grad_tokens = both_halves(
        grad_middle + norm_back(tok, scale_a, gain_a, summed(normed_parts))
    )
    grad_down_weight = assemble(
        down_grad_kernel, down_part, [((shard, down_weight.shape[0]), f32)]
    )[0]
    grad_qkv_weight, grad_out_weight, sums, rest = assemble(
        attention_weight_grad_kernel,
        att_part,
        [
            (qkv_weight.shape, f32),
            ((shard, qcols), f32),
            ((16, qkv_weight.shape[1]), f32),
            ((16, 4 * HEAD), f32),
        ],
    )
    split_at = qcols + HEAD
    own_bias = lax.dynamic_slice(sums, (0, f * (split_at // 8)), (1, split_at // 8))
    own_value = lax.dynamic_slice(sums, (0, split_at + f * (HEAD // 8)), (1, HEAD // 8))
    gain_sums = jnp.stack(
        [
            jnp.sum(grad_qkv_weight * qkv_weight.astype(f32), axis=1) / norm_attn.astype(f32),
            rest[1, :shard] / norm_mlp.astype(f32),
        ]
    )
    gain_sums = gain_sums + lax.ppermute(gain_sums, "tp", TP_SWAP)

    return (
        output,
        grad_tokens,
        gain_sums[0],
        grad_qkv_weight,
        own_bias,
        own_value,
        grad_out_weight.T,
        gain_sums[1],
        grad_gu_weight,
        grad_down_weight.T,
    )


def solution(mesh):
    in_specs = (
        P(("fsdp", "ctx"), None),
        P(("fsdp", "ctx"), None),
        P("fsdp"),
        P("fsdp", "tp"),
        P("tp", "fsdp"),
        P("tp", "fsdp"),
        P("fsdp"),
        P("fsdp", None, "tp"),
        P("tp", "fsdp"),
        P("fsdp", None),
        P("fsdp", None),
    )
    out_specs = (
        P(("fsdp", "ctx"), None),
        P(("fsdp", "ctx"), None),
        P("fsdp"),
        P("fsdp", "tp"),
        P("tp", "fsdp"),
        P("tp", "fsdp"),
        P("tp", "fsdp"),
        P("fsdp"),
        P("fsdp", None, "tp"),
        P("tp", "fsdp"),
    )
    return jax.shard_map(
        on_device, mesh=mesh, in_specs=in_specs, out_specs=out_specs, check_vma=False
    )
```

```python
import jax
import jax.numpy as jnp
from jax import lax
from jax.experimental import pallas as pl
from jax.experimental.pallas import tpu as pltpu
from jax.sharding import PartitionSpec as P

HEAD = 128
GROUP_Q = 6
EPS = 1e-06
THETA = 1000000.0

bf16 = jnp.bfloat16
f32 = jnp.float32

BLOCK = 128
ROWS = 256
GRAD_ROWS = 64
VMEM_BYTES = 60 * 2**20
VMEM_PART = 32 * 2**20
COST = pl.CostEstimate(flops=10**6, bytes_accessed=10**5, transcendentals=0)

TP_SWAP = [(0, 1), (1, 0)]
XH_SWAP = [(i, i ^ 4) for i in range(8)]
XL_SWAP = [(i, i ^ 1) for i in range(8)]
Y_GROUPS = [[0, 1, 2, 3], [4, 5, 6, 7]]
Z_GROUPS = [[0, 2, 4, 6], [1, 3, 5, 7]]


def y_shift(k):
    return [(h * 4 + y, h * 4 + (y + k) % 4) for h in range(2) for y in range(4)]


def contract(left, right, left_dim, right_dim):
    return lax.dot_general(
        left, right, (((left_dim,), (right_dim,)), ((), ())), preferred_element_type=f32
    )


def tie(*values):
    return lax.optimization_barrier(values)


def ordered(own, other, place):
    return jnp.stack([jnp.where(place == 0, own, other), jnp.where(place == 0, other, own)])


def gather(own, axis):
    copies = jnp.broadcast_to(own[None], (8,) + own.shape)
    return lax.all_to_all(copies, axis, 0, 0, tiled=True)


def spread(part, axis):
    return lax.all_to_all(part, axis, 0, 0, tiled=True)


def spread_along_z(part):
    return lax.all_to_all(part, "ctx", 0, 0, tiled=True, axis_index_groups=Z_GROUPS)


def summed(parts):
    return jnp.sum(parts.astype(f32), axis=0)


def gather_small(own, far):
    me = lax.axis_index("fsdp")
    hi, y = me // 4, me % 4
    out = jnp.zeros((8,) + own.shape, own.dtype)
    for d, base in ((0, own), (1, far)):
        out = lax.dynamic_update_index_in_dim(out, base, (hi ^ d) * 4 + y, 0)
        for k in (1, 3, 2):
            piece = lax.ppermute(base, "fsdp", y_shift(k))
            out = lax.dynamic_update_index_in_dim(out, piece, (hi ^ d) * 4 + (y - k + 4) % 4, 0)
    return out


def gather_along_y(own):
    return lax.all_gather(own, "fsdp", axis=0, axis_index_groups=Y_GROUPS, tiled=True)


def reduce_along_y(part):
    pair = lax.psum_scatter(
        part, "fsdp", scatter_dimension=0, axis_index_groups=Y_GROUPS, tiled=True
    )
    return pair.reshape(2, -1, part.shape[1])


def swap_over_hi(pair):
    hi = lax.axis_index("fsdp") // 4
    sent = jnp.where(hi == 0, pair[1], pair[0])
    return jnp.where(hi == 0, pair[0], pair[1]), lax.ppermute(sent, "fsdp", XH_SWAP)


def added(kept, got):
    return (kept.astype(f32) + got.astype(f32)).astype(bf16)


def gather_along_z(own):
    return lax.all_gather(own, "ctx", axis=0, axis_index_groups=Z_GROUPS)


def both_cores(mine):
    mine = mine.reshape(-1, mine.shape[-1])
    return [mine, lax.ppermute(mine, "tp", TP_SWAP)]


def pair_sums(mine, other):
    got = lax.ppermute(other, "tp", TP_SWAP)
    total = (mine.astype(f32) + got.astype(f32)).astype(bf16)
    return total.reshape(8, -1, total.shape[1])


def both_halves(own):
    t = lax.axis_index("tp")
    other = lax.ppermute(own, "tp", TP_SWAP)
    first = jnp.where(t == 0, own, other)
    second = jnp.where(t == 0, other, own)
    return jnp.concatenate([first, second], axis=0)


def rope_in(values, cosine, sine):
    return values * cosine + pltpu.roll(values, HEAD // 2, 1) * sine


def rope_out(grads, cosine, sine):
    return grads * cosine - pltpu.roll(grads, HEAD // 2, 1) * sine


def masked_scores(query, key, ends, places):
    scores = contract(query, key, 1, 1) * HEAD ** (-0.5)
    first, last = ends[:, :1], ends[:, HEAD // 2 : HEAD // 2 + 1]
    return jnp.where((places >= first) & (places <= last), scores, -1e30)


def attention_kernel(
    mine, other, gain, att, bias, cosine, sine, ends, places,
    query, key, value, attended, log_total, branch_mine, branch_other, weight,
):
    shard = weight.shape[0] // 8
    for i in range(8):
        weight[i * shard : (i + 1) * shard, :] = att[i, :shard, :]
    for i in range(4):
        at = slice(i * ROWS, (i + 1) * ROWS)
        half = slice(i % 2 * ROWS, (i % 2 + 1) * ROWS)
        rows = (mine if i < 2 else other)[half, :]
        normed = (rows.astype(f32) * gain[...]).astype(bf16)
        qkv = contract(normed, weight[:, : 3 * HEAD], 1, 0) + bias[...]
        query[at, :] = rope_in(qkv[:, :HEAD], cosine[at, :], sine[at, :]).astype(bf16)
        key[at, :] = rope_in(qkv[:, HEAD : 2 * HEAD], cosine[at, :], sine[at, :]).astype(bf16)
        value[at, :] = qkv[:, 2 * HEAD :].astype(bf16)
    for i in range(4):
        at = slice(i * ROWS, (i + 1) * ROWS)
        half = slice(i % 2 * ROWS, (i % 2 + 1) * ROWS)
        scores = masked_scores(query[at, :], key[...], ends[at, :], places[...])
        top = jnp.max(scores, axis=1, keepdims=True)
        raised = jnp.exp(scores - top)
        total = jnp.sum(raised, axis=1, keepdims=True)
        log_total[at, :] = top + jnp.log(total)
        probs = (raised / total).astype(bf16)
        rows = contract(probs, value[...], 1, 0).astype(bf16)
        attended[at, :] = rows
        branch = contract(rows, weight[:, 3 * HEAD :], 1, 1).astype(bf16)
        (branch_mine if i < 2 else branch_other)[half, :] = branch


def attention_grad_kernel(
    branch_mine, branch_other, mine, other, gain, att, query, key, value, attended, log_total,
    cosine, sine, ends, places,
    normed_mine, normed_other, grads, weight, normed, grad_qkv, grad_key, grad_value,
):
    shard = weight.shape[0] // 8
    for i in range(8):
        weight[i * shard : (i + 1) * shard, :] = att[i, :shard, :]
    for i in range(4):
        at = slice(i * ROWS, (i + 1) * ROWS)
        half = slice(i % 2 * ROWS, (i % 2 + 1) * ROWS)
        rows = (mine if i < 2 else other)[half, :]
        normed[at, :] = (rows.astype(f32) * gain[...]).astype(bf16)
        branch = (branch_mine if i < 2 else branch_other)[half, :]
        grad_att = contract(branch, weight[:, 3 * HEAD :], 1, 0).astype(bf16)
        scores = masked_scores(query[at, :], key[...], ends[at, :], places[...])
        probs = jnp.exp(scores - log_total[at, :])
        grad_probs = contract(grad_att, value[...], 1, 1)
        inner = jnp.sum(probs * grad_probs, axis=1, keepdims=True)
        grad_scores = (probs * (grad_probs - inner)).astype(bf16)
        grad_query = contract(grad_scores, key[...], 1, 0) * HEAD ** (-0.5)
        grad_qkv[at, :HEAD] = rope_out(grad_query, cosine[at, :], sine[at, :]).astype(bf16)
        key_part = contract(grad_scores, query[at, :], 0, 0)
        value_part = contract(probs.astype(bf16), grad_att, 0, 0)
        if i == 0:
            grad_key[...] = key_part
            grad_value[...] = value_part
        else:
            grad_key[...] += key_part
            grad_value[...] += value_part
    grad_key_pre = rope_out(grad_key[...] * HEAD ** (-0.5), cosine[...], sine[...])
    grad_qkv[:, HEAD : 2 * HEAD] = grad_key_pre.astype(bf16)
    grad_qkv[:, 2 * HEAD :] = grad_value[...].astype(bf16)
    for i in range(4):
        at = slice(i * ROWS, (i + 1) * ROWS)
        half = slice(i % 2 * ROWS, (i % 2 + 1) * ROWS)
        rows = contract(grad_qkv[at, :], weight[:, : 3 * HEAD], 1, 1).astype(bf16)
        (normed_mine if i < 2 else normed_other)[half, :] = rows
    sums = jnp.sum(grad_qkv[...].astype(f32), axis=0, keepdims=True)
    sums = jnp.concatenate([sums, jnp.zeros((1, HEAD), f32)], axis=1)
    pad = jnp.where(lax.broadcasted_iota(jnp.int32, (16, 4 * HEAD), 0) == 0, sums, 0.0).astype(bf16)
    top = attended[: 2 * ROWS, :]
    low = attended[2 * ROWS :, :]
    for i in range(4):
        cols = slice(2 * i * shard, 2 * (i + 1) * shard)
        qkv_part = contract(normed[:, cols], grad_qkv[...], 0, 0)
        out_part = contract(branch_mine[:, cols], top, 0, 0)
        out_part += contract(branch_other[:, cols], low, 0, 0)
        both = jnp.concatenate([qkv_part, out_part], axis=1).astype(bf16)
        for j in range(2):
            base = (2 * i + j) * (shard + 16)
            grads[base : base + shard, :] = both[j * shard : (j + 1) * shard, :]
            grads[base + shard : base + shard + 16, :] = pad


def ffn_kernel(hi, rows, grad, weight_own, weight_far, hidden, grad_gu, grad_rows):
    width = weight_own.shape[0]
    units = weight_own.shape[1] // 3
    at_own = pl.ds(pl.multiple_of(hi[0] * width, HEAD), width)
    at_far = pl.ds(pl.multiple_of((1 - hi[0]) * width, HEAD), width)

    def product(left, cols):
        return contract(left[:, at_own], weight_own[:, cols], 1, 0) + contract(
            left[:, at_far], weight_far[:, cols], 1, 0
        )

    gate = product(rows, slice(0, units))
    upward = product(rows, slice(units, 2 * units))
    sigmoid = jax.nn.sigmoid(gate)
    activated = gate * sigmoid
    hidden[...] = (activated * upward).astype(bf16)
    grad_hidden = product(grad, slice(2 * units, 3 * units))
    grad_gu[:, :units] = (
        grad_hidden * upward * sigmoid * (1.0 + gate * (1.0 - sigmoid))
    ).astype(bf16)
    grad_gu[:, units:] = (grad_hidden * activated).astype(bf16)
    for at, weight in ((at_own, weight_own), (at_far, weight_far)):
        grad_rows[:, at] = contract(grad_gu[...], weight[:, : 2 * units], 1, 1).astype(bf16)


def weight_grad_kernel(left_mine, left_other, right_mine, right_other, out):
    shard = left_mine.shape[1] // 8
    for i in range(4):
        cols = slice(2 * i * shard, 2 * (i + 1) * shard)
        part = contract(left_mine[:, cols], right_mine[...], 0, 0)
        part += contract(left_other[:, cols], right_other[...], 0, 0)
        for j in range(2):
            base = ((2 * i + j) % 4 * 2 + (2 * i + j) // 4) * shard
            out[base : base + shard, :] = part[j * shard : (j + 1) * shard, :].astype(bf16)


def output_kernel(hi, mine, other, weight_own, weight_far, out_mine, out_other):
    width = weight_own.shape[0]
    units = mine.shape[1]
    for weight, place in ((weight_own, hi[0]), (weight_far, 1 - hi[0])):
        at = pl.ds(pl.multiple_of(place * width, HEAD), width)
        for rows, out in ((other, out_other), (mine, out_mine)):
            out[:, at] = contract(rows[...], weight[:, 2 * units :], 1, 1).astype(bf16)


def down_grad_kernel(parts, out):
    start = 0
    for i in range(8):
        cols = (4 if i < 5 else 5) * BLOCK
        out[:, start : start + cols] = parts[i, :, :cols].astype(f32)
        start += cols


def gate_up_grad_kernel(parts, out):
    units = parts.shape[2] // 2
    start = 0
    for i in range(8):
        for j in range(4 if i < 5 else 5):
            for k in range(2):
                cols = slice(k * units + j * BLOCK, k * units + (j + 1) * BLOCK)
                out[:, k, start : start + BLOCK] = parts[i, :, cols].astype(f32)
            start += BLOCK


def attention_weight_grad_kernel(parts, grad_qkv, grad_out, sums, rest):
    shard = grad_qkv.shape[0]
    base = parts.shape[1] - shard - 16
    at = slice(base, base + shard)
    tail = slice(base + shard, base + shard + 16)
    qcols = GROUP_Q * HEAD
    pairs = 0.0
    tails = 0.0
    for i in range(GROUP_Q):
        cols = slice(i * HEAD, (i + 1) * HEAD)
        grad_qkv[:, cols] = parts[i, at, :HEAD].astype(f32)
        grad_out[:, cols] = parts[i, at, 3 * HEAD :].astype(f32)
        last = parts[i, tail, :].astype(f32)
        sums[:, cols] = last[:, :HEAD]
        pairs += parts[i, at, HEAD : 3 * HEAD].astype(f32)
        tails += last[:, HEAD : 3 * HEAD]
    grad_qkv[:, qcols:] = pairs
    sums[:, qcols:] = tails
    rest[...] = sum(parts[i, tail, :].astype(f32) for i in range(8))


def local_call(kernel, outs, scratch=(), limit=VMEM_PART):
    return pl.pallas_call(
        kernel,
        out_shape=[jax.ShapeDtypeStruct(shape, dtype) for shape, dtype in outs],
        scratch_shapes=[pltpu.VMEM(shape, dtype) for shape, dtype in scratch],
        compiler_params=pltpu.CompilerParams(vmem_limit_bytes=limit),
        cost_estimate=COST,
    )


def assemble(kernel, parts, outs):
    return local_call(kernel, outs)(parts)


def attention(mine, other, gain, att, bias, cosine, sine, ends, places):
    half, width = mine.shape
    outs = [((2 * half, HEAD), bf16)] * 4 + [((2 * half, 1), f32)] + [((half, width), bf16)] * 2
    return local_call(attention_kernel, outs, [((width, 4 * HEAD), bf16)], VMEM_BYTES)(
        mine, other, gain, att, bias, cosine, sine, ends, places
    )


def attention_grad(branch_mine, branch_other, mine, other, gain, att, *rest):
    half, width = mine.shape
    outs = [((half, width), bf16)] * 2 + [((width + 8 * 16, 4 * HEAD), bf16)]
    scratch = [
        ((width, 4 * HEAD), bf16),
        ((2 * half, width), bf16),
        ((2 * half, 3 * HEAD), bf16),
        ((2 * half, HEAD), f32),
        ((2 * half, HEAD), f32),
    ]
    return local_call(attention_grad_kernel, outs, scratch, VMEM_BYTES)(
        branch_mine, branch_other, mine, other, gain, att, *rest
    )


def weight_grad(lefts, rights):
    outs = [((lefts[0].shape[1], rights[0].shape[1]), bf16)]
    return local_call(weight_grad_kernel, outs)(*lefts, *rights)[0]


def output_rows(hi, rows, weight_own, weight_far):
    shape = (rows[0].shape[0], 2 * weight_own.shape[0])
    whole = [pl.BlockSpec(memory_space=pltpu.VMEM)] * 4
    return pl.pallas_call(
        output_kernel,
        in_specs=[pl.BlockSpec(memory_space=pltpu.SMEM)] + whole,
        out_specs=[pl.BlockSpec(memory_space=pltpu.VMEM)] * 2,
        out_shape=[jax.ShapeDtypeStruct(shape, bf16)] * 2,
        compiler_params=pltpu.CompilerParams(vmem_limit_bytes=VMEM_PART),
        cost_estimate=COST,
    )(hi, *rows, weight_own, weight_far)


def feed_forward(hi, rows, grad, weight_own, weight_far):
    count, width = rows.shape
    units = weight_own.shape[1] // 3

    def by_rows(cols):
        return pl.BlockSpec((ROWS, cols), lambda i, hi: (i, 0))

    whole = pl.BlockSpec(weight_own.shape, lambda i, hi: (0, 0))
    return pl.pallas_call(
        ffn_kernel,
        grid_spec=pltpu.PrefetchScalarGridSpec(
            num_scalar_prefetch=1,
            grid=(count // ROWS,),
            in_specs=[by_rows(width), by_rows(width), whole, whole],
            out_specs=[by_rows(units), by_rows(2 * units), by_rows(width)],
        ),
        out_shape=[
            jax.ShapeDtypeStruct((count, cols), bf16) for cols in (units, 2 * units, width)
        ],
        compiler_params=pltpu.CompilerParams(vmem_limit_bytes=VMEM_PART),
        cost_estimate=COST,
    )(hi, rows, grad, weight_own, weight_far)


def sequence_of(places, seq_lengths):
    ends = jnp.cumsum(seq_lengths)
    starts = ends - seq_lengths
    inside = (places[:, None] >= starts[None, :]) & (places[:, None] < ends[None, :])
    return jnp.sum(inside.astype(jnp.int32) * starts[None, :], axis=1)


def rotary(offset):
    half = HEAD // 2
    freqs = THETA ** (-(2.0 * jnp.arange(half, dtype=f32)) / HEAD)
    angle = offset.astype(f32)[:, None] * freqs[None, :]
    cosine, sine = jnp.cos(angle), jnp.sin(angle)
    return jnp.concatenate([cosine, cosine], axis=1), jnp.concatenate([-sine, sine], axis=1)


def rms_scale(values):
    return lax.rsqrt(jnp.mean(values * values, axis=-1, keepdims=True) + EPS)


def norm_back(values, scale, gain, incoming):
    weighted = incoming * gain
    return scale * weighted - values * scale**3 * jnp.mean(
        weighted * values, axis=-1, keepdims=True
    )


def on_device(
    tokens,
    cotangent,
    norm_attn,
    qkv_weight,
    qkv_bias,
    out_weight,
    norm_mlp,
    gate_up_weight,
    down_weight,
    lengths,
    deal,
):
    f = lax.axis_index("fsdp")
    c = lax.axis_index("ctx")
    t = lax.axis_index("tp")
    count, width = tokens.shape
    own = count // 2
    shard = qkv_weight.shape[0]
    qcols = GROUP_Q * HEAD
    has_head = c < GROUP_Q
    head = jnp.minimum(c, GROUP_Q - 1)

    tok = lax.dynamic_slice_in_dim(tokens, t * own, own)
    cot = lax.dynamic_slice_in_dim(cotangent, t * own, own)
    scale_a = rms_scale(tok)
    unit_own = (tok * scale_a).astype(bf16)
    grad_own = cot.astype(bf16)

    w_out_own = lax.dynamic_slice_in_dim(out_weight, head * HEAD, HEAD).T
    w_out_own = jnp.where(has_head, w_out_own, jnp.zeros_like(w_out_own))
    att_own = jnp.concatenate(
        [
            lax.dynamic_slice_in_dim(qkv_weight, head * HEAD, HEAD, axis=1),
            qkv_weight[:, qcols:],
            w_out_own,
        ],
        axis=1,
    )
    row = jnp.concatenate([norm_attn, norm_mlp, qkv_bias[0]])[None]
    att_own = jnp.concatenate([att_own, row, jnp.zeros((15, row.shape[1]), bf16)], axis=0)
    att_far = lax.ppermute(att_own, "fsdp", XH_SWAP)

    start = jnp.maximum(4 * c, 5 * c - 5) * BLOCK
    units = 5 * BLOCK
    gu_own = lax.dynamic_slice_in_dim(gate_up_weight, start, units, axis=2)
    inside = (jnp.arange(units) < 4 * BLOCK) | (c >= 5)
    gu_own = jnp.where(inside, gu_own, jnp.zeros_like(gu_own))
    down_own = lax.dynamic_slice_in_dim(down_weight, start, units).T
    ffn_own = jnp.concatenate([gu_own[:, 0], gu_own[:, 1], down_own], axis=1)

    att_all = gather_small(att_own, att_far)
    extra = att_all[:, shard].astype(f32)
    gain_a = extra[:, :shard].reshape(1, width)
    gain_m = extra[:, shard : 2 * shard].reshape(1, width)
    bias_all = extra[:, 2 * shard :].reshape(1, -1)
    bias = jnp.concatenate(
        [lax.dynamic_slice_in_dim(bias_all, head * HEAD, HEAD, axis=1), bias_all[:, qcols:]], axis=1
    )

    deal_all = deal[0].reshape(8, 2, own)[:, t ^ jnp.arange(2)]
    places = jnp.transpose(deal_all, (1, 0, 2)).reshape(-1)
    first = sequence_of(places, lengths[0])
    cosine, sine = rotary(places - first)
    ends = jnp.where(jnp.arange(HEAD) < HEAD // 2, first[:, None], places[:, None])
    order = (cosine, sine, ends, places[None, :])

    grad_pair = ordered(grad_own, lax.ppermute(grad_own, "ctx", XL_SWAP), c % 2)
    grad_copies = jnp.broadcast_to(grad_pair[None], (4,) + grad_pair.shape)
    unit_mine, att_all, grad_copies, ffn_own, *order = tie(
        gather(unit_own, "ctx"), att_all, grad_copies, ffn_own, *order
    )
    ffn_far = lax.ppermute(ffn_own, "fsdp", XH_SWAP)
    ffn_line = gather_along_y(ffn_own)
    grad_mine = spread_along_z(grad_copies)
    units_all = both_cores(unit_mine)
    held = attention(*units_all, gain_a, att_all, bias, *order)
    *held, grad_mine, ffn_far = tie(*held, grad_mine, ffn_far)
    query, key, value, attended, log_total, branch_mine, branch_other = held
    ffn_far = gather_along_y(ffn_far)
    branch_parts = pair_sums(branch_mine, branch_other)
    grads = both_cores(grad_mine)
    branch = summed(spread(branch_parts, "ctx"))
    middle = tok + branch
    scale_m = rms_scale(middle)
    normed2_mine = gather((middle * scale_m * gain_m).astype(bf16), "ctx")
    normed2 = both_cores(normed2_mine)

    hi = (f // 4)[None]
    hidden, grad_gu, parts = zip(
        *[feed_forward(hi, r, g, ffn_line, ffn_far) for r, g in zip(normed2, grads)]
    )
    parts = pair_sums(*parts)
    parts, *held = tie(parts, *normed2, *grad_gu, *hidden, *grads)
    normed2, grad_gu, hidden, grads = held[0:2], held[2:4], held[4:6], held[6:8]
    normed2_parts = spread(parts, "ctx")

    gu_blocks, *held = tie(weight_grad(normed2, grad_gu), *grads, *hidden)
    grads, hidden = held[:2], held[2:]
    gu_sums = reduce_along_y(gu_blocks)
    normed2_parts, down_blocks, *output_raw = tie(
        normed2_parts,
        weight_grad(grads, hidden),
        *output_rows(hi, hidden, ffn_line, ffn_far),
    )
    down_sums = reduce_along_y(down_blocks)

    grad_middle = cot + norm_back(middle, scale_m, gain_m, summed(normed2_parts))
    output_parts = pair_sums(*output_raw)
    gu_kept, gu_got = swap_over_hi(gu_sums)
    branch_mine, gu_kept, gu_got, output_parts = tie(
        gather(grad_middle.astype(bf16), "ctx"), gu_kept, gu_got, output_parts
    )
    output_parts = spread_along_z(output_parts.reshape(4, 2 * own, width))
    gu_share = added(gu_kept, gu_got)
    gu_far = lax.ppermute(gu_share, "ctx", XL_SWAP)
    grad_branch = both_cores(branch_mine)
    normed_mine, normed_other, att_grads = attention_grad(
        *grad_branch, *units_all, gain_a, att_all, query, key, value, attended, log_total, *order
    )
    att_grads, gu_share, gu_far, output_parts = tie(att_grads, gu_share, gu_far, output_parts)
    att_parts = spread(att_grads.reshape(8, -1, 4 * HEAD), "fsdp")
    gu_part = gather_along_z(ordered(gu_share, gu_far, c % 2)).reshape(8, shard, -1)
    normed_parts = pair_sums(normed_mine, normed_other)
    normed_parts, down_sums, output_parts, gu_share = tie(
        normed_parts, down_sums, output_parts, gu_share
    )
    down_kept, down_got = swap_over_hi(down_sums)
    output_pair = summed(output_parts).reshape(2, own, width)
    gain_part = jnp.sum(gu_share.astype(f32) * ffn_own[:, : 2 * units].astype(f32), axis=1)
    gain_row = jnp.pad(gain_part.astype(bf16)[None], ((shard + 1, 14), (0, 4 * HEAD - shard)))
    output_kept = jnp.where(c % 2 == 0, output_pair[0], output_pair[1])
    output_sent = jnp.where(c % 2 == 0, output_pair[1], output_pair[0]).astype(bf16)
    att_parts, down_kept, down_got, gain_row, normed_parts, output_kept, output_sent = tie(
        att_parts, down_kept, down_got, gain_row, normed_parts, output_kept, output_sent
    )
    att_share = (summed(att_parts) + gain_row).astype(bf16)
    thirds = [normed_parts[:, :, i * 4 * HEAD : (i + 1) * 4 * HEAD] for i in range(3)]
    packed = jnp.concatenate(
        thirds + [jnp.broadcast_to(att_share[None], (8,) + att_share.shape)], axis=1
    )
    down_share = added(down_kept, down_got)
    down_far = lax.ppermute(down_share, "ctx", XL_SWAP)
    output_got = lax.ppermute(output_sent, "ctx", XL_SWAP)
    packed, down_share, down_far, output_got = tie(packed, down_share, down_far, output_got)
    down_part = gather_along_z(ordered(down_share, down_far, c % 2)).reshape(8, shard, units)
    output = both_halves(middle + output_kept + output_got.astype(f32))
    grad_gu_weight = pl.pallas_call(
        gate_up_grad_kernel,
        grid=(shard // GRAD_ROWS,),
        in_specs=[pl.BlockSpec((8, GRAD_ROWS, 2 * units), lambda i: (0, i, 0))],
        out_specs=pl.BlockSpec((GRAD_ROWS,) + gate_up_weight.shape[1:], lambda i: (i, 0, 0)),
        out_shape=jax.ShapeDtypeStruct(gate_up_weight.shape, f32),
        compiler_params=pltpu.CompilerParams(vmem_limit_bytes=VMEM_PART),
        cost_estimate=COST,
    )(gu_part)
    att_part, grad_gu_weight, output = tie(spread(packed, "ctx"), grad_gu_weight, output)
    grad_normed = jnp.concatenate(
        [summed(att_part[:, i * own : (i + 1) * own]) for i in range(3)], axis=1
    )
    grad_tokens = both_halves(grad_middle + norm_back(tok, scale_a, gain_a, grad_normed))
    grad_qkv_weight, grad_out_weight, sums, rest = assemble(
        attention_weight_grad_kernel,
        att_part,
        [
            (qkv_weight.shape, f32),
            ((shard, qcols), f32),
            ((16, qkv_weight.shape[1]), f32),
            ((16, 4 * HEAD), f32),
        ],
    )
    sums, rest, down_part = tie(sums, rest, down_part)
    grad_down_weight = assemble(
        down_grad_kernel, down_part, [((shard, down_weight.shape[0]), f32)]
    )[0]
    split_at = qcols + HEAD
    own_bias = lax.dynamic_slice(sums, (0, f * (split_at // 8)), (1, split_at // 8))
    own_value = lax.dynamic_slice(sums, (0, split_at + f * (HEAD // 8)), (1, HEAD // 8))
    gain_sums = jnp.stack(
        [
            jnp.sum(grad_qkv_weight * qkv_weight.astype(f32), axis=1) / norm_attn.astype(f32),
            rest[1, :shard] / norm_mlp.astype(f32),
        ]
    )
    gain_sums = gain_sums + lax.ppermute(gain_sums, "tp", TP_SWAP)

    return (
        output,
        grad_tokens,
        gain_sums[0],
        grad_qkv_weight,
        own_bias,
        own_value,
        grad_out_weight.T,
        gain_sums[1],
        grad_gu_weight,
        grad_down_weight.T,
    )


def solution(mesh):
    in_specs = (
        P(("fsdp", "ctx"), None),
        P(("fsdp", "ctx"), None),
        P("fsdp"),
        P("fsdp", "tp"),
        P("tp", "fsdp"),
        P("tp", "fsdp"),
        P("fsdp"),
        P("fsdp", None, "tp"),
        P("tp", "fsdp"),
        P("fsdp", None),
        P("fsdp", None),
    )
    out_specs = (
        P(("fsdp", "ctx"), None),
        P(("fsdp", "ctx"), None),
        P("fsdp"),
        P("fsdp", "tp"),
        P("tp", "fsdp"),
        P("tp", "fsdp"),
        P("tp", "fsdp"),
        P("fsdp"),
        P("fsdp", None, "tp"),
        P("tp", "fsdp"),
    )
    return jax.shard_map(
        on_device, mesh=mesh, in_specs=in_specs, out_specs=out_specs, check_vma=False
    )
```

```python
import jax
import jax.numpy as jnp
from jax import lax
from jax.experimental import pallas as pl
from jax.experimental.pallas import tpu as pltpu
from jax.sharding import PartitionSpec as P

HEAD = 128
GROUP_Q = 6
EPS = 1e-06
THETA = 1000000.0

bf16 = jnp.bfloat16
f32 = jnp.float32

BLOCK = 128
ROWS = 256
GRAD_ROWS = 64
VMEM_BYTES = 60 * 2**20
VMEM_PART = 32 * 2**20
COST = pl.CostEstimate(flops=10**6, bytes_accessed=10**5, transcendentals=0)

TP_SWAP = [(0, 1), (1, 0)]
XH_SWAP = [(i, i ^ 4) for i in range(8)]
XL_SWAP = [(i, i ^ 1) for i in range(8)]
Y_GROUPS = [[0, 1, 2, 3], [4, 5, 6, 7]]
Z_GROUPS = [[0, 2, 4, 6], [1, 3, 5, 7]]


def y_shift(k):
    return [(h * 4 + y, h * 4 + (y + k) % 4) for h in range(2) for y in range(4)]


def contract(left, right, left_dim, right_dim):
    return lax.dot_general(
        left, right, (((left_dim,), (right_dim,)), ((), ())), preferred_element_type=f32
    )


def tie(*values):
    return lax.optimization_barrier(values)


def ordered(own, other, place):
    return jnp.stack([jnp.where(place == 0, own, other), jnp.where(place == 0, other, own)])


def gather(own, axis):
    copies = jnp.broadcast_to(own[None], (8,) + own.shape)
    return lax.all_to_all(copies, axis, 0, 0, tiled=True)


def spread(part, axis):
    return lax.all_to_all(part, axis, 0, 0, tiled=True)


def spread_along_z(part):
    return lax.all_to_all(part, "ctx", 0, 0, tiled=True, axis_index_groups=Z_GROUPS)


def summed(parts):
    return jnp.sum(parts.astype(f32), axis=0)


def gather_small(own, far):
    me = lax.axis_index("fsdp")
    hi, y = me // 4, me % 4
    out = jnp.zeros((8,) + own.shape, own.dtype)
    for d, base in ((0, own), (1, far)):
        out = lax.dynamic_update_index_in_dim(out, base, (hi ^ d) * 4 + y, 0)
        for k in (1, 3, 2):
            piece = lax.ppermute(base, "fsdp", y_shift(k))
            out = lax.dynamic_update_index_in_dim(out, piece, (hi ^ d) * 4 + (y - k + 4) % 4, 0)
    return out


def gather_along_y(own):
    return lax.all_gather(own, "fsdp", axis=0, axis_index_groups=Y_GROUPS, tiled=True)


def reduce_along_y(part):
    pair = lax.psum_scatter(
        part, "fsdp", scatter_dimension=0, axis_index_groups=Y_GROUPS, tiled=True
    )
    return pair.reshape(2, -1, part.shape[1])


def swap_over_hi(pair):
    hi = lax.axis_index("fsdp") // 4
    sent = jnp.where(hi == 0, pair[1], pair[0])
    return jnp.where(hi == 0, pair[0], pair[1]), lax.ppermute(sent, "fsdp", XH_SWAP)


def added(kept, got):
    return (kept.astype(f32) + got.astype(f32)).astype(bf16)


def gather_along_z(own):
    return lax.all_gather(own, "ctx", axis=0, axis_index_groups=Z_GROUPS)


def both_cores(mine):
    mine = mine.reshape(-1, mine.shape[-1])
    return [mine, lax.ppermute(mine, "tp", TP_SWAP)]


def pair_sums(mine, other):
    got = lax.ppermute(other, "tp", TP_SWAP)
    total = (mine.astype(f32) + got.astype(f32)).astype(bf16)
    return total.reshape(8, -1, total.shape[1])


def both_halves(own):
    t = lax.axis_index("tp")
    other = lax.ppermute(own, "tp", TP_SWAP)
    first = jnp.where(t == 0, own, other)
    second = jnp.where(t == 0, other, own)
    return jnp.concatenate([first, second], axis=0)


def rope_in(values, cosine, sine):
    return values * cosine + pltpu.roll(values, HEAD // 2, 1) * sine


def rope_out(grads, cosine, sine):
    return grads * cosine - pltpu.roll(grads, HEAD // 2, 1) * sine


def masked_scores(query, key, ends, places):
    scores = contract(query, key, 1, 1) * HEAD ** (-0.5)
    first, last = ends[:, :1], ends[:, HEAD // 2 : HEAD // 2 + 1]
    return jnp.where((places >= first) & (places <= last), scores, -1e30)


def attention_kernel(
    mine, other, gain, att, bias, cosine, sine, ends, places,
    query, key, value, attended, log_total, branch_mine, branch_other, weight,
):
    shard = weight.shape[0] // 8
    for i in range(8):
        weight[i * shard : (i + 1) * shard, :] = att[i, :shard, :]
    for i in range(4):
        at = slice(i * ROWS, (i + 1) * ROWS)
        half = slice(i % 2 * ROWS, (i % 2 + 1) * ROWS)
        rows = (mine if i < 2 else other)[half, :]
        normed = (rows.astype(f32) * gain[...]).astype(bf16)
        qkv = contract(normed, weight[:, : 3 * HEAD], 1, 0) + bias[...]
        query[at, :] = rope_in(qkv[:, :HEAD], cosine[at, :], sine[at, :]).astype(bf16)
        key[at, :] = rope_in(qkv[:, HEAD : 2 * HEAD], cosine[at, :], sine[at, :]).astype(bf16)
        value[at, :] = qkv[:, 2 * HEAD :].astype(bf16)
    for i in range(4):
        at = slice(i * ROWS, (i + 1) * ROWS)
        half = slice(i % 2 * ROWS, (i % 2 + 1) * ROWS)
        scores = masked_scores(query[at, :], key[...], ends[at, :], places[...])
        top = jnp.max(scores, axis=1, keepdims=True)
        raised = jnp.exp(scores - top)
        total = jnp.sum(raised, axis=1, keepdims=True)
        log_total[at, :] = top + jnp.log(total)
        probs = (raised / total).astype(bf16)
        rows = contract(probs, value[...], 1, 0).astype(bf16)
        attended[at, :] = rows
        branch = contract(rows, weight[:, 3 * HEAD :], 1, 1).astype(bf16)
        (branch_mine if i < 2 else branch_other)[half, :] = branch


def attention_grad_kernel(
    branch_mine, branch_other, mine, other, gain, att, query, key, value, attended, log_total,
    cosine, sine, ends, places,
    normed_mine, normed_other, grads, weight, normed, grad_qkv, grad_key, grad_value,
):
    shard = weight.shape[0] // 8
    for i in range(8):
        weight[i * shard : (i + 1) * shard, :] = att[i, :shard, :]
    for i in range(4):
        at = slice(i * ROWS, (i + 1) * ROWS)
        half = slice(i % 2 * ROWS, (i % 2 + 1) * ROWS)
        rows = (mine if i < 2 else other)[half, :]
        normed[at, :] = (rows.astype(f32) * gain[...]).astype(bf16)
        branch = (branch_mine if i < 2 else branch_other)[half, :]
        grad_att = contract(branch, weight[:, 3 * HEAD :], 1, 0).astype(bf16)
        scores = masked_scores(query[at, :], key[...], ends[at, :], places[...])
        probs = jnp.exp(scores - log_total[at, :])
        grad_probs = contract(grad_att, value[...], 1, 1)
        inner = jnp.sum(probs * grad_probs, axis=1, keepdims=True)
        grad_scores = (probs * (grad_probs - inner)).astype(bf16)
        grad_query = contract(grad_scores, key[...], 1, 0) * HEAD ** (-0.5)
        grad_qkv[at, :HEAD] = rope_out(grad_query, cosine[at, :], sine[at, :]).astype(bf16)
        key_part = contract(grad_scores, query[at, :], 0, 0)
        value_part = contract(probs.astype(bf16), grad_att, 0, 0)
        if i == 0:
            grad_key[...] = key_part
            grad_value[...] = value_part
        else:
            grad_key[...] += key_part
            grad_value[...] += value_part
    grad_key_pre = rope_out(grad_key[...] * HEAD ** (-0.5), cosine[...], sine[...])
    grad_qkv[:, HEAD : 2 * HEAD] = grad_key_pre.astype(bf16)
    grad_qkv[:, 2 * HEAD :] = grad_value[...].astype(bf16)
    for i in range(4):
        at = slice(i * ROWS, (i + 1) * ROWS)
        half = slice(i % 2 * ROWS, (i % 2 + 1) * ROWS)
        rows = contract(grad_qkv[at, :], weight[:, : 3 * HEAD], 1, 1).astype(bf16)
        (normed_mine if i < 2 else normed_other)[half, :] = rows
    sums = jnp.sum(grad_qkv[...].astype(f32), axis=0, keepdims=True)
    sums = jnp.concatenate([sums, jnp.zeros((1, HEAD), f32)], axis=1)
    pad = jnp.where(lax.broadcasted_iota(jnp.int32, (16, 4 * HEAD), 0) == 0, sums, 0.0).astype(bf16)
    top = attended[: 2 * ROWS, :]
    low = attended[2 * ROWS :, :]
    for i in range(4):
        cols = slice(2 * i * shard, 2 * (i + 1) * shard)
        qkv_part = contract(normed[:, cols], grad_qkv[...], 0, 0)
        out_part = contract(branch_mine[:, cols], top, 0, 0)
        out_part += contract(branch_other[:, cols], low, 0, 0)
        both = jnp.concatenate([qkv_part, out_part], axis=1).astype(bf16)
        for j in range(2):
            base = (2 * i + j) * (shard + 16)
            grads[base : base + shard, :] = both[j * shard : (j + 1) * shard, :]
            grads[base + shard : base + shard + 16, :] = pad


def ffn_kernel(hi, rows, grad, weight_own, weight_far, hidden, grad_gu, grad_rows):
    width = weight_own.shape[0]
    units = weight_own.shape[1] // 3
    at_own = pl.ds(pl.multiple_of(hi[0] * width, HEAD), width)
    at_far = pl.ds(pl.multiple_of((1 - hi[0]) * width, HEAD), width)

    def product(left, cols):
        return contract(left[:, at_own], weight_own[:, cols], 1, 0) + contract(
            left[:, at_far], weight_far[:, cols], 1, 0
        )

    gate = product(rows, slice(0, units))
    upward = product(rows, slice(units, 2 * units))
    sigmoid = jax.nn.sigmoid(gate)
    activated = gate * sigmoid
    hidden[...] = (activated * upward).astype(bf16)
    grad_hidden = product(grad, slice(2 * units, 3 * units))
    grad_gu[:, :units] = (
        grad_hidden * upward * sigmoid * (1.0 + gate * (1.0 - sigmoid))
    ).astype(bf16)
    grad_gu[:, units:] = (grad_hidden * activated).astype(bf16)
    for at, weight in ((at_own, weight_own), (at_far, weight_far)):
        grad_rows[:, at] = contract(grad_gu[...], weight[:, : 2 * units], 1, 1).astype(bf16)


def weight_grad_kernel(left_mine, left_other, right_mine, right_other, out):
    shard = left_mine.shape[1] // 8
    for i in range(4):
        cols = slice(2 * i * shard, 2 * (i + 1) * shard)
        part = contract(left_mine[:, cols], right_mine[...], 0, 0)
        part += contract(left_other[:, cols], right_other[...], 0, 0)
        for j in range(2):
            base = ((2 * i + j) % 4 * 2 + (2 * i + j) // 4) * shard
            out[base : base + shard, :] = part[j * shard : (j + 1) * shard, :].astype(bf16)


def output_kernel(hi, mine, other, weight_own, weight_far, out_mine, out_other):
    width = weight_own.shape[0]
    units = mine.shape[1]
    for weight, place in ((weight_own, hi[0]), (weight_far, 1 - hi[0])):
        at = pl.ds(pl.multiple_of(place * width, HEAD), width)
        for rows, out in ((other, out_other), (mine, out_mine)):
            out[:, at] = contract(rows[...], weight[:, 2 * units :], 1, 1).astype(bf16)


def down_grad_kernel(parts, out):
    start = 0
    for i in range(8):
        cols = (4 if i < 5 else 5) * BLOCK
        out[:, start : start + cols] = parts[i, :, :cols].astype(f32)
        start += cols


def gate_up_grad_kernel(parts, out):
    units = parts.shape[2] // 2
    start = 0
    for i in range(8):
        for j in range(4 if i < 5 else 5):
            for k in range(2):
                cols = slice(k * units + j * BLOCK, k * units + (j + 1) * BLOCK)
                out[:, k, start : start + BLOCK] = parts[i, :, cols].astype(f32)
            start += BLOCK


def attention_weight_grad_kernel(parts, grad_qkv, grad_out, sums, rest):
    shard = grad_qkv.shape[0]
    base = parts.shape[1] - shard - 16
    at = slice(base, base + shard)
    tail = slice(base + shard, base + shard + 16)
    qcols = GROUP_Q * HEAD
    pairs = 0.0
    tails = 0.0
    for i in range(GROUP_Q):
        cols = slice(i * HEAD, (i + 1) * HEAD)
        grad_qkv[:, cols] = parts[i, at, :HEAD].astype(f32)
        grad_out[:, cols] = parts[i, at, 3 * HEAD :].astype(f32)
        last = parts[i, tail, :].astype(f32)
        sums[:, cols] = last[:, :HEAD]
        pairs += parts[i, at, HEAD : 3 * HEAD].astype(f32)
        tails += last[:, HEAD : 3 * HEAD]
    grad_qkv[:, qcols:] = pairs
    sums[:, qcols:] = tails
    rest[...] = sum(parts[i, tail, :].astype(f32) for i in range(8))


def local_call(kernel, outs, scratch=(), limit=VMEM_PART):
    return pl.pallas_call(
        kernel,
        out_shape=[jax.ShapeDtypeStruct(shape, dtype) for shape, dtype in outs],
        scratch_shapes=[pltpu.VMEM(shape, dtype) for shape, dtype in scratch],
        compiler_params=pltpu.CompilerParams(vmem_limit_bytes=limit),
        cost_estimate=COST,
    )


def assemble(kernel, parts, outs):
    return local_call(kernel, outs)(parts)


def attention(mine, other, gain, att, bias, cosine, sine, ends, places):
    half, width = mine.shape
    outs = [((2 * half, HEAD), bf16)] * 4 + [((2 * half, 1), f32)] + [((half, width), bf16)] * 2
    return local_call(attention_kernel, outs, [((width, 4 * HEAD), bf16)], VMEM_BYTES)(
        mine, other, gain, att, bias, cosine, sine, ends, places
    )


def attention_grad(branch_mine, branch_other, mine, other, gain, att, *rest):
    half, width = mine.shape
    outs = [((half, width), bf16)] * 2 + [((width + 8 * 16, 4 * HEAD), bf16)]
    scratch = [
        ((width, 4 * HEAD), bf16),
        ((2 * half, width), bf16),
        ((2 * half, 3 * HEAD), bf16),
        ((2 * half, HEAD), f32),
        ((2 * half, HEAD), f32),
    ]
    return local_call(attention_grad_kernel, outs, scratch, VMEM_BYTES)(
        branch_mine, branch_other, mine, other, gain, att, *rest
    )


def weight_grad(lefts, rights):
    outs = [((lefts[0].shape[1], rights[0].shape[1]), bf16)]
    return local_call(weight_grad_kernel, outs)(*lefts, *rights)[0]


def output_rows(hi, rows, weight_own, weight_far):
    shape = (rows[0].shape[0], 2 * weight_own.shape[0])
    whole = [pl.BlockSpec(memory_space=pltpu.VMEM)] * 4
    return pl.pallas_call(
        output_kernel,
        in_specs=[pl.BlockSpec(memory_space=pltpu.SMEM)] + whole,
        out_specs=[pl.BlockSpec(memory_space=pltpu.VMEM)] * 2,
        out_shape=[jax.ShapeDtypeStruct(shape, bf16)] * 2,
        compiler_params=pltpu.CompilerParams(vmem_limit_bytes=VMEM_PART),
        cost_estimate=COST,
    )(hi, *rows, weight_own, weight_far)


def feed_forward(hi, rows, grad, weight_own, weight_far):
    count, width = rows.shape
    units = weight_own.shape[1] // 3

    def by_rows(cols):
        return pl.BlockSpec((ROWS, cols), lambda i, hi: (i, 0))

    whole = pl.BlockSpec(weight_own.shape, lambda i, hi: (0, 0))
    return pl.pallas_call(
        ffn_kernel,
        grid_spec=pltpu.PrefetchScalarGridSpec(
            num_scalar_prefetch=1,
            grid=(count // ROWS,),
            in_specs=[by_rows(width), by_rows(width), whole, whole],
            out_specs=[by_rows(units), by_rows(2 * units), by_rows(width)],
        ),
        out_shape=[
            jax.ShapeDtypeStruct((count, cols), bf16) for cols in (units, 2 * units, width)
        ],
        compiler_params=pltpu.CompilerParams(vmem_limit_bytes=VMEM_PART),
        cost_estimate=COST,
    )(hi, rows, grad, weight_own, weight_far)


def sequence_of(places, seq_lengths):
    ends = jnp.cumsum(seq_lengths)
    starts = ends - seq_lengths
    inside = (places[:, None] >= starts[None, :]) & (places[:, None] < ends[None, :])
    return jnp.sum(inside.astype(jnp.int32) * starts[None, :], axis=1)


def rotary(offset):
    half = HEAD // 2
    freqs = THETA ** (-(2.0 * jnp.arange(half, dtype=f32)) / HEAD)
    angle = offset.astype(f32)[:, None] * freqs[None, :]
    cosine, sine = jnp.cos(angle), jnp.sin(angle)
    return jnp.concatenate([cosine, cosine], axis=1), jnp.concatenate([-sine, sine], axis=1)


def rms_scale(values):
    return lax.rsqrt(jnp.mean(values * values, axis=-1, keepdims=True) + EPS)


def norm_back(values, scale, gain, incoming):
    weighted = incoming * gain
    return scale * weighted - values * scale**3 * jnp.mean(
        weighted * values, axis=-1, keepdims=True
    )


def on_device(
    tokens,
    cotangent,
    norm_attn,
    qkv_weight,
    qkv_bias,
    out_weight,
    norm_mlp,
    gate_up_weight,
    down_weight,
    lengths,
    deal,
):
    f = lax.axis_index("fsdp")
    c = lax.axis_index("ctx")
    t = lax.axis_index("tp")
    count, width = tokens.shape
    own = count // 2
    shard = qkv_weight.shape[0]
    qcols = GROUP_Q * HEAD
    has_head = c < GROUP_Q
    head = jnp.minimum(c, GROUP_Q - 1)

    tok = lax.dynamic_slice_in_dim(tokens, t * own, own)
    cot = lax.dynamic_slice_in_dim(cotangent, t * own, own)
    scale_a = rms_scale(tok)
    unit_own = (tok * scale_a).astype(bf16)
    grad_own = cot.astype(bf16)

    w_out_own = lax.dynamic_slice_in_dim(out_weight, head * HEAD, HEAD).T
    w_out_own = jnp.where(has_head, w_out_own, jnp.zeros_like(w_out_own))
    att_own = jnp.concatenate(
        [
            lax.dynamic_slice_in_dim(qkv_weight, head * HEAD, HEAD, axis=1),
            qkv_weight[:, qcols:],
            w_out_own,
        ],
        axis=1,
    )
    row = jnp.concatenate([norm_attn, norm_mlp, qkv_bias[0]])[None]
    att_own = jnp.concatenate([att_own, row, jnp.zeros((15, row.shape[1]), bf16)], axis=0)
    att_far = lax.ppermute(att_own, "fsdp", XH_SWAP)

    start = jnp.maximum(4 * c, 5 * c - 5) * BLOCK
    units = 5 * BLOCK
    gu_own = lax.dynamic_slice_in_dim(gate_up_weight, start, units, axis=2)
    inside = (jnp.arange(units) < 4 * BLOCK) | (c >= 5)
    gu_own = jnp.where(inside, gu_own, jnp.zeros_like(gu_own))
    down_own = lax.dynamic_slice_in_dim(down_weight, start, units).T
    ffn_own = jnp.concatenate([gu_own[:, 0], gu_own[:, 1], down_own], axis=1)

    att_all = gather_small(att_own, att_far)
    extra = att_all[:, shard].astype(f32)
    gain_a = extra[:, :shard].reshape(1, width)
    gain_m = extra[:, shard : 2 * shard].reshape(1, width)
    bias_all = extra[:, 2 * shard :].reshape(1, -1)
    bias = jnp.concatenate(
        [lax.dynamic_slice_in_dim(bias_all, head * HEAD, HEAD, axis=1), bias_all[:, qcols:]], axis=1
    )

    deal_all = deal[0].reshape(8, 2, own)[:, t ^ jnp.arange(2)]
    places = jnp.transpose(deal_all, (1, 0, 2)).reshape(-1)
    first = sequence_of(places, lengths[0])
    cosine, sine = rotary(places - first)
    ends = jnp.where(jnp.arange(HEAD) < HEAD // 2, first[:, None], places[:, None])
    order = (cosine, sine, ends, places[None, :])

    grad_pair = ordered(grad_own, lax.ppermute(grad_own, "ctx", XL_SWAP), c % 2)
    grad_copies = jnp.broadcast_to(grad_pair[None], (4,) + grad_pair.shape)
    unit_mine, att_all, grad_copies, ffn_own, *order = tie(
        gather(unit_own, "ctx"), att_all, grad_copies, ffn_own, *order
    )
    ffn_far = lax.ppermute(ffn_own, "fsdp", XH_SWAP)
    ffn_line = gather_along_y(ffn_own)
    grad_mine = spread_along_z(grad_copies)
    units_all = both_cores(unit_mine)
    held = attention(*units_all, gain_a, att_all, bias, *order)
    *held, grad_mine, ffn_far = tie(*held, grad_mine, ffn_far)
    query, key, value, attended, log_total, branch_mine, branch_other = held
    ffn_far = gather_along_y(ffn_far)
    branch_parts = pair_sums(branch_mine, branch_other)
    grads = both_cores(grad_mine)
    branch = summed(spread(branch_parts, "ctx"))
    middle = tok + branch
    scale_m = rms_scale(middle)
    normed2_mine = gather((middle * scale_m * gain_m).astype(bf16), "ctx")
    normed2 = both_cores(normed2_mine)

    hi = (f // 4)[None]
    hidden, grad_gu, parts = zip(
        *[feed_forward(hi, r, g, ffn_line, ffn_far) for r, g in zip(normed2, grads)]
    )
    parts = pair_sums(*parts)
    parts, *held = tie(parts, *normed2, *grad_gu, *hidden, *grads)
    normed2, grad_gu, hidden, grads = held[0:2], held[2:4], held[4:6], held[6:8]
    normed2_parts = spread(parts, "ctx")

    gu_blocks, *held = tie(weight_grad(normed2, grad_gu), *grads, *hidden)
    grads, hidden = held[:2], held[2:]
    gu_sums = reduce_along_y(gu_blocks)
    normed2_parts, down_blocks, *output_raw = tie(
        normed2_parts,
        weight_grad(grads, hidden),
        *output_rows(hi, hidden, ffn_line, ffn_far),
    )
    down_sums = reduce_along_y(down_blocks)

    grad_middle = cot + norm_back(middle, scale_m, gain_m, summed(normed2_parts))
    branch_low = grad_middle.astype(bf16)
    branch_pair = ordered(branch_low, lax.ppermute(branch_low, "ctx", XL_SWAP), c % 2)
    branch_spread = spread_along_z(jnp.broadcast_to(branch_pair[None], (4,) + branch_pair.shape))
    output_parts = pair_sums(*output_raw)
    gu_kept, gu_got = swap_over_hi(gu_sums)
    branch_mine, gu_kept, gu_got, output_parts = tie(
        branch_spread, gu_kept, gu_got, output_parts
    )
    output_parts = spread_along_z(output_parts.reshape(4, 2 * own, width))
    gu_share = added(gu_kept, gu_got)
    gu_far = lax.ppermute(gu_share, "ctx", XL_SWAP)
    grad_branch = both_cores(branch_mine)
    normed_mine, normed_other, att_grads = attention_grad(
        *grad_branch, *units_all, gain_a, att_all, query, key, value, attended, log_total, *order
    )
    att_grads, gu_share, gu_far, output_parts = tie(att_grads, gu_share, gu_far, output_parts)
    att_parts = spread(att_grads.reshape(8, -1, 4 * HEAD), "fsdp")
    gu_part = gather_along_z(ordered(gu_share, gu_far, c % 2)).reshape(8, shard, -1)
    normed_parts = pair_sums(normed_mine, normed_other)
    normed_parts, down_sums, output_parts, gu_share = tie(
        normed_parts, down_sums, output_parts, gu_share
    )
    down_kept, down_got = swap_over_hi(down_sums)
    output_pair = summed(output_parts).reshape(2, own, width)
    gain_part = jnp.sum(gu_share.astype(f32) * ffn_own[:, : 2 * units].astype(f32), axis=1)
    gain_row = jnp.pad(gain_part.astype(bf16)[None], ((shard + 1, 14), (0, 4 * HEAD - shard)))
    output_kept = jnp.where(c % 2 == 0, output_pair[0], output_pair[1])
    output_sent = jnp.where(c % 2 == 0, output_pair[1], output_pair[0]).astype(bf16)
    att_parts, down_kept, down_got, gain_row, normed_parts, output_kept, output_sent = tie(
        att_parts, down_kept, down_got, gain_row, normed_parts, output_kept, output_sent
    )
    att_share = (summed(att_parts) + gain_row).astype(bf16)
    thirds = [normed_parts[:, :, i * 4 * HEAD : (i + 1) * 4 * HEAD] for i in range(3)]
    packed = jnp.concatenate(
        thirds + [jnp.broadcast_to(att_share[None], (8,) + att_share.shape)], axis=1
    )
    down_share = added(down_kept, down_got)
    down_far = lax.ppermute(down_share, "ctx", XL_SWAP)
    output_got = lax.ppermute(output_sent, "ctx", XL_SWAP)
    packed, down_share, down_far, output_got = tie(packed, down_share, down_far, output_got)
    down_part = gather_along_z(ordered(down_share, down_far, c % 2)).reshape(8, shard, units)
    output = both_halves(middle + output_kept + output_got.astype(f32))
    grad_gu_weight = pl.pallas_call(
        gate_up_grad_kernel,
        grid=(shard // GRAD_ROWS,),
        in_specs=[pl.BlockSpec((8, GRAD_ROWS, 2 * units), lambda i: (0, i, 0))],
        out_specs=pl.BlockSpec((GRAD_ROWS,) + gate_up_weight.shape[1:], lambda i: (i, 0, 0)),
        out_shape=jax.ShapeDtypeStruct(gate_up_weight.shape, f32),
        compiler_params=pltpu.CompilerParams(vmem_limit_bytes=VMEM_PART),
        cost_estimate=COST,
    )(gu_part)
    att_part, grad_gu_weight, output = tie(spread(packed, "ctx"), grad_gu_weight, output)
    grad_normed = jnp.concatenate(
        [summed(att_part[:, i * own : (i + 1) * own]) for i in range(3)], axis=1
    )
    grad_tokens = both_halves(grad_middle + norm_back(tok, scale_a, gain_a, grad_normed))
    grad_qkv_weight, grad_out_weight, sums, rest = assemble(
        attention_weight_grad_kernel,
        att_part,
        [
            (qkv_weight.shape, f32),
            ((shard, qcols), f32),
            ((16, qkv_weight.shape[1]), f32),
            ((16, 4 * HEAD), f32),
        ],
    )
    sums, rest, down_part = tie(sums, rest, down_part)
    grad_down_weight = assemble(
        down_grad_kernel, down_part, [((shard, down_weight.shape[0]), f32)]
    )[0]
    split_at = qcols + HEAD
    own_bias = lax.dynamic_slice(sums, (0, f * (split_at // 8)), (1, split_at // 8))
    own_value = lax.dynamic_slice(sums, (0, split_at + f * (HEAD // 8)), (1, HEAD // 8))
    gain_sums = jnp.stack(
        [
            jnp.sum(grad_qkv_weight * qkv_weight.astype(f32), axis=1) / norm_attn.astype(f32),
            rest[1, :shard] / norm_mlp.astype(f32),
        ]
    )
    gain_sums = gain_sums + lax.ppermute(gain_sums, "tp", TP_SWAP)

    return (
        output,
        grad_tokens,
        gain_sums[0],
        grad_qkv_weight,
        own_bias,
        own_value,
        grad_out_weight.T,
        gain_sums[1],
        grad_gu_weight,
        grad_down_weight.T,
    )


def solution(mesh):
    in_specs = (
        P(("fsdp", "ctx"), None),
        P(("fsdp", "ctx"), None),
        P("fsdp"),
        P("fsdp", "tp"),
        P("tp", "fsdp"),
        P("tp", "fsdp"),
        P("fsdp"),
        P("fsdp", None, "tp"),
        P("tp", "fsdp"),
        P("fsdp", None),
        P("fsdp", None),
    )
    out_specs = (
        P(("fsdp", "ctx"), None),
        P(("fsdp", "ctx"), None),
        P("fsdp"),
        P("fsdp", "tp"),
        P("tp", "fsdp"),
        P("tp", "fsdp"),
        P("tp", "fsdp"),
        P("fsdp"),
        P("fsdp", None, "tp"),
        P("tp", "fsdp"),
    )
    return jax.shard_map(
        on_device, mesh=mesh, in_specs=in_specs, out_specs=out_specs, check_vma=False
    )
```

```python
import jax
import jax.numpy as jnp
from jax import lax
from jax.experimental import pallas as pl
from jax.experimental.pallas import tpu as pltpu
from jax.sharding import PartitionSpec as P

HEAD = 128
GROUP_Q = 6
EPS = 1e-06
THETA = 1000000.0

bf16 = jnp.bfloat16
f32 = jnp.float32

BLOCK = 128
ROWS = 256
GRAD_ROWS = 64
VMEM_BYTES = 60 * 2**20
VMEM_PART = 32 * 2**20
COST = pl.CostEstimate(flops=10**6, bytes_accessed=10**5, transcendentals=0)

TP_SWAP = [(0, 1), (1, 0)]
XH_SWAP = [(i, i ^ 4) for i in range(8)]
XL_SWAP = [(i, i ^ 1) for i in range(8)]
Y_GROUPS = [[0, 1, 2, 3], [4, 5, 6, 7]]
Z_GROUPS = [[0, 2, 4, 6], [1, 3, 5, 7]]


def y_shift(k):
    return [(h * 4 + y, h * 4 + (y + k) % 4) for h in range(2) for y in range(4)]


def contract(left, right, left_dim, right_dim):
    return lax.dot_general(
        left, right, (((left_dim,), (right_dim,)), ((), ())), preferred_element_type=f32
    )


def tie(*values):
    return lax.optimization_barrier(values)


def ordered(own, other, place):
    return jnp.stack([jnp.where(place == 0, own, other), jnp.where(place == 0, other, own)])


def gather(own, axis):
    copies = jnp.broadcast_to(own[None], (8,) + own.shape)
    return lax.all_to_all(copies, axis, 0, 0, tiled=True)


def spread(part, axis):
    return lax.all_to_all(part, axis, 0, 0, tiled=True)


def spread_along_z(part):
    return lax.all_to_all(part, "ctx", 0, 0, tiled=True, axis_index_groups=Z_GROUPS)


def summed(parts):
    return jnp.sum(parts.astype(f32), axis=0)


def gather_small(own, far):
    me = lax.axis_index("fsdp")
    hi, y = me // 4, me % 4
    out = jnp.zeros((8,) + own.shape, own.dtype)
    for d, base in ((0, own), (1, far)):
        out = lax.dynamic_update_index_in_dim(out, base, (hi ^ d) * 4 + y, 0)
        for k in (1, 3, 2):
            piece = lax.ppermute(base, "fsdp", y_shift(k))
            out = lax.dynamic_update_index_in_dim(out, piece, (hi ^ d) * 4 + (y - k + 4) % 4, 0)
    return out


def gather_along_y(own):
    return lax.all_gather(own, "fsdp", axis=0, axis_index_groups=Y_GROUPS, tiled=True)


def reduce_along_y(part):
    pair = lax.psum_scatter(
        part, "fsdp", scatter_dimension=0, axis_index_groups=Y_GROUPS, tiled=True
    )
    return pair.reshape(2, -1, part.shape[1])


def swap_over_hi(pair):
    hi = lax.axis_index("fsdp") // 4
    sent = jnp.where(hi == 0, pair[1], pair[0])
    return jnp.where(hi == 0, pair[0], pair[1]), lax.ppermute(sent, "fsdp", XH_SWAP)


def added(kept, got):
    return (kept.astype(f32) + got.astype(f32)).astype(bf16)


def gather_along_z(own):
    return lax.all_gather(own, "ctx", axis=0, axis_index_groups=Z_GROUPS)


def both_cores(mine):
    mine = mine.reshape(-1, mine.shape[-1])
    return [mine, lax.ppermute(mine, "tp", TP_SWAP)]


def pair_sums(mine, other):
    got = lax.ppermute(other, "tp", TP_SWAP)
    total = (mine.astype(f32) + got.astype(f32)).astype(bf16)
    return total.reshape(8, -1, total.shape[1])


def both_halves(own):
    t = lax.axis_index("tp")
    other = lax.ppermute(own, "tp", TP_SWAP)
    first = jnp.where(t == 0, own, other)
    second = jnp.where(t == 0, other, own)
    return jnp.concatenate([first, second], axis=0)


def rope_in(values, cosine, sine):
    return values * cosine + pltpu.roll(values, HEAD // 2, 1) * sine


def rope_out(grads, cosine, sine):
    return grads * cosine - pltpu.roll(grads, HEAD // 2, 1) * sine


def masked_scores(query, key, ends, places):
    scores = contract(query, key, 1, 1) * HEAD ** (-0.5)
    first, last = ends[:, :1], ends[:, HEAD // 2 : HEAD // 2 + 1]
    return jnp.where((places >= first) & (places <= last), scores, -1e30)


def attention_kernel(
    mine, other, gain, att, bias, cosine, sine, ends, places,
    query, key, value, attended, log_total, branch_mine, branch_other, weight,
):
    shard = weight.shape[0] // 8
    for i in range(8):
        weight[i * shard : (i + 1) * shard, :] = att[i, :shard, :]
    for i in range(4):
        at = slice(i * ROWS, (i + 1) * ROWS)
        half = slice(i % 2 * ROWS, (i % 2 + 1) * ROWS)
        rows = (mine if i < 2 else other)[half, :]
        normed = (rows.astype(f32) * gain[...]).astype(bf16)
        qkv = contract(normed, weight[:, : 3 * HEAD], 1, 0) + bias[...]
        query[at, :] = rope_in(qkv[:, :HEAD], cosine[at, :], sine[at, :]).astype(bf16)
        key[at, :] = rope_in(qkv[:, HEAD : 2 * HEAD], cosine[at, :], sine[at, :]).astype(bf16)
        value[at, :] = qkv[:, 2 * HEAD :].astype(bf16)
    for i in range(4):
        at = slice(i * ROWS, (i + 1) * ROWS)
        half = slice(i % 2 * ROWS, (i % 2 + 1) * ROWS)
        scores = masked_scores(query[at, :], key[...], ends[at, :], places[...])
        top = jnp.max(scores, axis=1, keepdims=True)
        raised = jnp.exp(scores - top)
        total = jnp.sum(raised, axis=1, keepdims=True)
        log_total[at, :] = top + jnp.log(total)
        probs = (raised / total).astype(bf16)
        rows = contract(probs, value[...], 1, 0).astype(bf16)
        attended[at, :] = rows
        branch = contract(rows, weight[:, 3 * HEAD :], 1, 1).astype(bf16)
        (branch_mine if i < 2 else branch_other)[half, :] = branch


def attention_grad_kernel(
    branch_mine, branch_other, mine, other, gain, att, query, key, value, attended, log_total,
    cosine, sine, ends, places,
    normed_mine, normed_other, grads, weight, normed, grad_qkv, grad_key, grad_value,
):
    shard = weight.shape[0] // 8
    for i in range(8):
        weight[i * shard : (i + 1) * shard, :] = att[i, :shard, :]
    for i in range(4):
        at = slice(i * ROWS, (i + 1) * ROWS)
        half = slice(i % 2 * ROWS, (i % 2 + 1) * ROWS)
        rows = (mine if i < 2 else other)[half, :]
        normed[at, :] = (rows.astype(f32) * gain[...]).astype(bf16)
        branch = (branch_mine if i < 2 else branch_other)[half, :]
        grad_att = contract(branch, weight[:, 3 * HEAD :], 1, 0).astype(bf16)
        scores = masked_scores(query[at, :], key[...], ends[at, :], places[...])
        probs = jnp.exp(scores - log_total[at, :])
        grad_probs = contract(grad_att, value[...], 1, 1)
        inner = jnp.sum(probs * grad_probs, axis=1, keepdims=True)
        grad_scores = (probs * (grad_probs - inner)).astype(bf16)
        grad_query = contract(grad_scores, key[...], 1, 0) * HEAD ** (-0.5)
        grad_qkv[at, :HEAD] = rope_out(grad_query, cosine[at, :], sine[at, :]).astype(bf16)
        key_part = contract(grad_scores, query[at, :], 0, 0)
        value_part = contract(probs.astype(bf16), grad_att, 0, 0)
        if i == 0:
            grad_key[...] = key_part
            grad_value[...] = value_part
        else:
            grad_key[...] += key_part
            grad_value[...] += value_part
    grad_key_pre = rope_out(grad_key[...] * HEAD ** (-0.5), cosine[...], sine[...])
    grad_qkv[:, HEAD : 2 * HEAD] = grad_key_pre.astype(bf16)
    grad_qkv[:, 2 * HEAD :] = grad_value[...].astype(bf16)
    for i in range(4):
        at = slice(i * ROWS, (i + 1) * ROWS)
        half = slice(i % 2 * ROWS, (i % 2 + 1) * ROWS)
        rows = contract(grad_qkv[at, :], weight[:, : 3 * HEAD], 1, 1).astype(bf16)
        (normed_mine if i < 2 else normed_other)[half, :] = rows
    sums = jnp.sum(grad_qkv[...].astype(f32), axis=0, keepdims=True)
    sums = jnp.concatenate([sums, jnp.zeros((1, HEAD), f32)], axis=1)
    pad = jnp.where(lax.broadcasted_iota(jnp.int32, (16, 4 * HEAD), 0) == 0, sums, 0.0).astype(bf16)
    top = attended[: 2 * ROWS, :]
    low = attended[2 * ROWS :, :]
    for i in range(4):
        cols = slice(2 * i * shard, 2 * (i + 1) * shard)
        qkv_part = contract(normed[:, cols], grad_qkv[...], 0, 0)
        out_part = contract(branch_mine[:, cols], top, 0, 0)
        out_part += contract(branch_other[:, cols], low, 0, 0)
        both = jnp.concatenate([qkv_part, out_part], axis=1).astype(bf16)
        for j in range(2):
            base = (2 * i + j) * (shard + 16)
            grads[base : base + shard, :] = both[j * shard : (j + 1) * shard, :]
            grads[base + shard : base + shard + 16, :] = pad


def ffn_kernel(hi, rows, grad, weight_own, weight_far, hidden, grad_gu, grad_rows):
    width = weight_own.shape[0]
    units = weight_own.shape[1] // 3
    at_own = pl.ds(pl.multiple_of(hi[0] * width, HEAD), width)
    at_far = pl.ds(pl.multiple_of((1 - hi[0]) * width, HEAD), width)

    def product(left, cols):
        return contract(left[:, at_own], weight_own[:, cols], 1, 0) + contract(
            left[:, at_far], weight_far[:, cols], 1, 0
        )

    gate = product(rows, slice(0, units))
    upward = product(rows, slice(units, 2 * units))
    sigmoid = jax.nn.sigmoid(gate)
    activated = gate * sigmoid
    hidden[...] = (activated * upward).astype(bf16)
    grad_hidden = product(grad, slice(2 * units, 3 * units))
    grad_gu[:, :units] = (
        grad_hidden * upward * sigmoid * (1.0 + gate * (1.0 - sigmoid))
    ).astype(bf16)
    grad_gu[:, units:] = (grad_hidden * activated).astype(bf16)
    for at, weight in ((at_own, weight_own), (at_far, weight_far)):
        grad_rows[:, at] = contract(grad_gu[...], weight[:, : 2 * units], 1, 1).astype(bf16)


def weight_grad_kernel(left_mine, left_other, right_mine, right_other, out):
    shard = left_mine.shape[1] // 8
    for i in range(4):
        cols = slice(2 * i * shard, 2 * (i + 1) * shard)
        part = contract(left_mine[:, cols], right_mine[...], 0, 0)
        part += contract(left_other[:, cols], right_other[...], 0, 0)
        for j in range(2):
            base = ((2 * i + j) % 4 * 2 + (2 * i + j) // 4) * shard
            out[base : base + shard, :] = part[j * shard : (j + 1) * shard, :].astype(bf16)


def output_kernel(hi, mine, other, weight_own, weight_far, out_mine, out_other):
    width = weight_own.shape[0]
    units = mine.shape[1]
    for weight, place in ((weight_own, hi[0]), (weight_far, 1 - hi[0])):
        at = pl.ds(pl.multiple_of(place * width, HEAD), width)
        for rows, out in ((other, out_other), (mine, out_mine)):
            out[:, at] = contract(rows[...], weight[:, 2 * units :], 1, 1).astype(bf16)


def down_grad_kernel(parts, out):
    start = 0
    for i in range(8):
        cols = (4 if i < 5 else 5) * BLOCK
        out[:, start : start + cols] = parts[i, :, :cols].astype(f32)
        start += cols


def gate_up_grad_kernel(parts, out):
    units = parts.shape[2] // 2
    start = 0
    for i in range(8):
        for j in range(4 if i < 5 else 5):
            for k in range(2):
                cols = slice(k * units + j * BLOCK, k * units + (j + 1) * BLOCK)
                out[:, k, start : start + BLOCK] = parts[i, :, cols].astype(f32)
            start += BLOCK


def attention_weight_grad_kernel(parts, grad_qkv, grad_out, sums, rest):
    shard = grad_qkv.shape[0]
    base = parts.shape[1] - shard - 16
    at = slice(base, base + shard)
    tail = slice(base + shard, base + shard + 16)
    qcols = GROUP_Q * HEAD
    pairs = 0.0
    tails = 0.0
    for i in range(GROUP_Q):
        cols = slice(i * HEAD, (i + 1) * HEAD)
        grad_qkv[:, cols] = parts[i, at, :HEAD].astype(f32)
        grad_out[:, cols] = parts[i, at, 3 * HEAD :].astype(f32)
        last = parts[i, tail, :].astype(f32)
        sums[:, cols] = last[:, :HEAD]
        pairs += parts[i, at, HEAD : 3 * HEAD].astype(f32)
        tails += last[:, HEAD : 3 * HEAD]
    grad_qkv[:, qcols:] = pairs
    sums[:, qcols:] = tails
    rest[...] = sum(parts[i, tail, :].astype(f32) for i in range(8))


def local_call(kernel, outs, scratch=(), limit=VMEM_PART):
    return pl.pallas_call(
        kernel,
        out_shape=[jax.ShapeDtypeStruct(shape, dtype) for shape, dtype in outs],
        scratch_shapes=[pltpu.VMEM(shape, dtype) for shape, dtype in scratch],
        compiler_params=pltpu.CompilerParams(vmem_limit_bytes=limit),
        cost_estimate=COST,
    )


def assemble(kernel, parts, outs):
    return local_call(kernel, outs)(parts)


def attention(mine, other, gain, att, bias, cosine, sine, ends, places):
    half, width = mine.shape
    outs = [((2 * half, HEAD), bf16)] * 4 + [((2 * half, 1), f32)] + [((half, width), bf16)] * 2
    return local_call(attention_kernel, outs, [((width, 4 * HEAD), bf16)], VMEM_BYTES)(
        mine, other, gain, att, bias, cosine, sine, ends, places
    )


def attention_grad(branch_mine, branch_other, mine, other, gain, att, *rest):
    half, width = mine.shape
    outs = [((half, width), bf16)] * 2 + [((width + 8 * 16, 4 * HEAD), bf16)]
    scratch = [
        ((width, 4 * HEAD), bf16),
        ((2 * half, width), bf16),
        ((2 * half, 3 * HEAD), bf16),
        ((2 * half, HEAD), f32),
        ((2 * half, HEAD), f32),
    ]
    return local_call(attention_grad_kernel, outs, scratch, VMEM_BYTES)(
        branch_mine, branch_other, mine, other, gain, att, *rest
    )


def weight_grad(lefts, rights):
    outs = [((lefts[0].shape[1], rights[0].shape[1]), bf16)]
    return local_call(weight_grad_kernel, outs)(*lefts, *rights)[0]


def output_rows(hi, rows, weight_own, weight_far):
    shape = (rows[0].shape[0], 2 * weight_own.shape[0])
    whole = [pl.BlockSpec(memory_space=pltpu.VMEM)] * 4
    return pl.pallas_call(
        output_kernel,
        in_specs=[pl.BlockSpec(memory_space=pltpu.SMEM)] + whole,
        out_specs=[pl.BlockSpec(memory_space=pltpu.VMEM)] * 2,
        out_shape=[jax.ShapeDtypeStruct(shape, bf16)] * 2,
        compiler_params=pltpu.CompilerParams(vmem_limit_bytes=VMEM_PART),
        cost_estimate=COST,
    )(hi, *rows, weight_own, weight_far)


def feed_forward(hi, rows, grad, weight_own, weight_far):
    count, width = rows.shape
    units = weight_own.shape[1] // 3

    def by_rows(cols):
        return pl.BlockSpec((ROWS, cols), lambda i, hi: (i, 0))

    whole = pl.BlockSpec(weight_own.shape, lambda i, hi: (0, 0))
    return pl.pallas_call(
        ffn_kernel,
        grid_spec=pltpu.PrefetchScalarGridSpec(
            num_scalar_prefetch=1,
            grid=(count // ROWS,),
            in_specs=[by_rows(width), by_rows(width), whole, whole],
            out_specs=[by_rows(units), by_rows(2 * units), by_rows(width)],
        ),
        out_shape=[
            jax.ShapeDtypeStruct((count, cols), bf16) for cols in (units, 2 * units, width)
        ],
        compiler_params=pltpu.CompilerParams(vmem_limit_bytes=VMEM_PART),
        cost_estimate=COST,
    )(hi, rows, grad, weight_own, weight_far)


def sequence_of(places, seq_lengths):
    ends = jnp.cumsum(seq_lengths)
    starts = ends - seq_lengths
    inside = (places[:, None] >= starts[None, :]) & (places[:, None] < ends[None, :])
    return jnp.sum(inside.astype(jnp.int32) * starts[None, :], axis=1)


def rotary(offset):
    half = HEAD // 2
    freqs = THETA ** (-(2.0 * jnp.arange(half, dtype=f32)) / HEAD)
    angle = offset.astype(f32)[:, None] * freqs[None, :]
    cosine, sine = jnp.cos(angle), jnp.sin(angle)
    return jnp.concatenate([cosine, cosine], axis=1), jnp.concatenate([-sine, sine], axis=1)


def rms_scale(values):
    return lax.rsqrt(jnp.mean(values * values, axis=-1, keepdims=True) + EPS)


def norm_back(values, scale, gain, incoming):
    weighted = incoming * gain
    return scale * weighted - values * scale**3 * jnp.mean(
        weighted * values, axis=-1, keepdims=True
    )


def on_device(
    tokens,
    cotangent,
    norm_attn,
    qkv_weight,
    qkv_bias,
    out_weight,
    norm_mlp,
    gate_up_weight,
    down_weight,
    lengths,
    deal,
):
    f = lax.axis_index("fsdp")
    c = lax.axis_index("ctx")
    t = lax.axis_index("tp")
    count, width = tokens.shape
    own = count // 2
    shard = qkv_weight.shape[0]
    qcols = GROUP_Q * HEAD
    has_head = c < GROUP_Q
    head = jnp.minimum(c, GROUP_Q - 1)

    tok = lax.dynamic_slice_in_dim(tokens, t * own, own)
    cot = lax.dynamic_slice_in_dim(cotangent, t * own, own)
    scale_a = rms_scale(tok)
    unit_own = (tok * scale_a).astype(bf16)
    grad_own = cot.astype(bf16)

    w_out_own = lax.dynamic_slice_in_dim(out_weight, head * HEAD, HEAD).T
    w_out_own = jnp.where(has_head, w_out_own, jnp.zeros_like(w_out_own))
    att_own = jnp.concatenate(
        [
            lax.dynamic_slice_in_dim(qkv_weight, head * HEAD, HEAD, axis=1),
            qkv_weight[:, qcols:],
            w_out_own,
        ],
        axis=1,
    )
    row = jnp.concatenate([norm_attn, norm_mlp, qkv_bias[0]])[None]
    att_own = jnp.concatenate([att_own, row, jnp.zeros((15, row.shape[1]), bf16)], axis=0)
    att_far = lax.ppermute(att_own, "fsdp", XH_SWAP)

    start = jnp.maximum(4 * c, 5 * c - 5) * BLOCK
    units = 5 * BLOCK
    gu_own = lax.dynamic_slice_in_dim(gate_up_weight, start, units, axis=2)
    inside = (jnp.arange(units) < 4 * BLOCK) | (c >= 5)
    gu_own = jnp.where(inside, gu_own, jnp.zeros_like(gu_own))
    down_own = lax.dynamic_slice_in_dim(down_weight, start, units).T
    ffn_own = jnp.concatenate([gu_own[:, 0], gu_own[:, 1], down_own], axis=1)

    att_all = gather_small(att_own, att_far)
    extra = att_all[:, shard].astype(f32)
    gain_a = extra[:, :shard].reshape(1, width)
    gain_m = extra[:, shard : 2 * shard].reshape(1, width)
    bias_all = extra[:, 2 * shard :].reshape(1, -1)
    bias = jnp.concatenate(
        [lax.dynamic_slice_in_dim(bias_all, head * HEAD, HEAD, axis=1), bias_all[:, qcols:]], axis=1
    )

    deal_all = deal[0].reshape(8, 2, own)[:, t ^ jnp.arange(2)]
    places = jnp.transpose(deal_all, (1, 0, 2)).reshape(-1)
    first = sequence_of(places, lengths[0])
    cosine, sine = rotary(places - first)
    ends = jnp.where(jnp.arange(HEAD) < HEAD // 2, first[:, None], places[:, None])
    order = (cosine, sine, ends, places[None, :])

    grad_pair = ordered(grad_own, lax.ppermute(grad_own, "ctx", XL_SWAP), c % 2)
    grad_copies = jnp.broadcast_to(grad_pair[None], (4,) + grad_pair.shape)
    unit_mine, att_all, grad_copies, ffn_own, *order = tie(
        gather(unit_own, "ctx"), att_all, grad_copies, ffn_own, *order
    )
    ffn_far = lax.ppermute(ffn_own, "fsdp", XH_SWAP)
    ffn_line = gather_along_y(ffn_own)
    grad_mine = spread_along_z(grad_copies)
    units_all = both_cores(unit_mine)
    held = attention(*units_all, gain_a, att_all, bias, *order)
    *held, grad_mine, ffn_far = tie(*held, grad_mine, ffn_far)
    query, key, value, attended, log_total, branch_mine, branch_other = held
    ffn_far = gather_along_y(ffn_far)
    branch_parts = pair_sums(branch_mine, branch_other)
    grads = both_cores(grad_mine)
    branch = summed(spread(branch_parts, "ctx"))
    middle = tok + branch
    scale_m = rms_scale(middle)
    normed2_mine = gather((middle * scale_m * gain_m).astype(bf16), "ctx")
    normed2 = both_cores(normed2_mine)

    hi = (f // 4)[None]
    hidden, grad_gu, parts = zip(
        *[feed_forward(hi, r, g, ffn_line, ffn_far) for r, g in zip(normed2, grads)]
    )
    parts = pair_sums(*parts)
    parts, *held = tie(parts, *normed2, *grad_gu, *hidden, *grads)
    normed2, grad_gu, hidden, grads = held[0:2], held[2:4], held[4:6], held[6:8]
    normed2_parts = spread(parts, "ctx")

    gu_blocks, *held = tie(weight_grad(normed2, grad_gu), *grads, *hidden)
    grads, hidden = held[:2], held[2:]
    gu_sums = reduce_along_y(gu_blocks)
    normed2_parts, down_blocks, *output_raw = tie(
        normed2_parts,
        weight_grad(grads, hidden),
        *output_rows(hi, hidden, ffn_line, ffn_far),
    )
    down_sums = reduce_along_y(down_blocks)

    grad_middle = cot + norm_back(middle, scale_m, gain_m, summed(normed2_parts))
    branch_low = grad_middle.astype(bf16)
    branch_pair = ordered(branch_low, lax.ppermute(branch_low, "ctx", XL_SWAP), c % 2)
    branch_spread = spread_along_z(jnp.broadcast_to(branch_pair[None], (4,) + branch_pair.shape))
    output_parts = pair_sums(*output_raw)
    gu_kept, gu_got = swap_over_hi(gu_sums)
    branch_mine, gu_kept, gu_got, output_parts = tie(
        branch_spread, gu_kept, gu_got, output_parts
    )
    output_parts = spread_along_z(output_parts.reshape(4, 2 * own, width))
    gu_share = added(gu_kept, gu_got)
    gu_far = lax.ppermute(gu_share, "ctx", XL_SWAP)
    grad_branch = both_cores(branch_mine)
    normed_mine, normed_other, att_grads = attention_grad(
        *grad_branch, *units_all, gain_a, att_all, query, key, value, attended, log_total, *order
    )
    att_grads, gu_share, gu_far, output_parts = tie(att_grads, gu_share, gu_far, output_parts)
    att_parts = spread(att_grads.reshape(8, -1, 4 * HEAD), "fsdp")
    gu_part = gather_along_z(ordered(gu_share, gu_far, c % 2)).reshape(8, shard, -1)
    normed_parts = pair_sums(normed_mine, normed_other)
    normed_parts, down_sums, output_parts, gu_share = tie(
        normed_parts, down_sums, output_parts, gu_share
    )
    down_kept, down_got = swap_over_hi(down_sums)
    output_pair = summed(output_parts).reshape(2, own, width)
    gain_part = jnp.sum(gu_share.astype(f32) * ffn_own[:, : 2 * units].astype(f32), axis=1)
    gain_row = jnp.pad(gain_part.astype(bf16)[None], ((shard + 1, 14), (0, 4 * HEAD - shard)))
    output_kept = jnp.where(c % 2 == 0, output_pair[0], output_pair[1])
    output_sent = jnp.where(c % 2 == 0, output_pair[1], output_pair[0]).astype(bf16)
    att_parts, down_kept, down_got, gain_row, normed_parts, output_kept, output_sent = tie(
        att_parts, down_kept, down_got, gain_row, normed_parts, output_kept, output_sent
    )
    att_share = (summed(att_parts) + gain_row).astype(bf16)
    thirds = [normed_parts[:, :, i * 4 * HEAD : (i + 1) * 4 * HEAD] for i in range(3)]
    packed = jnp.concatenate(
        thirds + [jnp.broadcast_to(att_share[None], (8,) + att_share.shape)], axis=1
    )
    down_share = added(down_kept, down_got)
    down_far = lax.ppermute(down_share, "ctx", XL_SWAP)
    output_got = lax.ppermute(output_sent, "ctx", XL_SWAP)
    packed, down_share, down_far, output_got = tie(packed, down_share, down_far, output_got)
    down_part = gather_along_z(ordered(down_share, down_far, c % 2)).reshape(8, shard, units)
    output = both_halves(middle + output_kept + output_got.astype(f32))
    grad_gu_weight = pl.pallas_call(
        gate_up_grad_kernel,
        grid=(shard // GRAD_ROWS,),
        in_specs=[pl.BlockSpec((8, GRAD_ROWS, 2 * units), lambda i: (0, i, 0))],
        out_specs=pl.BlockSpec((GRAD_ROWS,) + gate_up_weight.shape[1:], lambda i: (i, 0, 0)),
        out_shape=jax.ShapeDtypeStruct(gate_up_weight.shape, f32),
        compiler_params=pltpu.CompilerParams(vmem_limit_bytes=VMEM_PART),
        cost_estimate=COST,
    )(gu_part)
    att_part, grad_gu_weight, output = tie(spread(packed, "ctx"), grad_gu_weight, output)
    grad_normed = jnp.concatenate(
        [summed(att_part[:, i * own : (i + 1) * own]) for i in range(3)], axis=1
    )
    grad_tokens = both_halves(grad_middle + norm_back(tok, scale_a, gain_a, grad_normed))
    grad_qkv_weight, grad_out_weight, sums, rest = assemble(
        attention_weight_grad_kernel,
        att_part,
        [
            (qkv_weight.shape, f32),
            ((shard, qcols), f32),
            ((16, qkv_weight.shape[1]), f32),
            ((16, 4 * HEAD), f32),
        ],
    )
    split_at = qcols + HEAD
    own_bias = lax.dynamic_slice(sums, (0, f * (split_at // 8)), (1, split_at // 8))
    own_value = lax.dynamic_slice(sums, (0, split_at + f * (HEAD // 8)), (1, HEAD // 8))
    gain_sums = jnp.stack(
        [
            jnp.sum(grad_qkv_weight * qkv_weight.astype(f32), axis=1) / norm_attn.astype(f32),
            rest[1, :shard] / norm_mlp.astype(f32),
        ]
    )
    gain_sums = gain_sums + lax.ppermute(gain_sums, "tp", TP_SWAP)
    gain_sums, grad_tokens, own_bias, own_value, down_part = tie(
        gain_sums, grad_tokens, own_bias, own_value, down_part
    )
    grad_down_weight = assemble(
        down_grad_kernel, down_part, [((shard, down_weight.shape[0]), f32)]
    )[0]

    return (
        output,
        grad_tokens,
        gain_sums[0],
        grad_qkv_weight,
        own_bias,
        own_value,
        grad_out_weight.T,
        gain_sums[1],
        grad_gu_weight,
        grad_down_weight.T,
    )


def solution(mesh):
    in_specs = (
        P(("fsdp", "ctx"), None),
        P(("fsdp", "ctx"), None),
        P("fsdp"),
        P("fsdp", "tp"),
        P("tp", "fsdp"),
        P("tp", "fsdp"),
        P("fsdp"),
        P("fsdp", None, "tp"),
        P("tp", "fsdp"),
        P("fsdp", None),
        P("fsdp", None),
    )
    out_specs = (
        P(("fsdp", "ctx"), None),
        P(("fsdp", "ctx"), None),
        P("fsdp"),
        P("fsdp", "tp"),
        P("tp", "fsdp"),
        P("tp", "fsdp"),
        P("tp", "fsdp"),
        P("fsdp"),
        P("fsdp", None, "tp"),
        P("tp", "fsdp"),
    )
    return jax.shard_map(
        on_device, mesh=mesh, in_specs=in_specs, out_specs=out_specs, check_vma=False
    )
```
